256 devices in a mesh: snp: 32 (over y, z), ind: 8 (over x, core).
Axes of the slice: x: 4, y: 4, z: 8, core: 2. Of those that a mesh axis runs over, the one named last changes fastest.
Arguments:
- beta_hat: float32 [64, 32768], P('ind', 'snp'), may hold values from -8 to 8
- ld_band: float32 [32768, 1024], P('snp'), as said below
- band_start: int32 [256], P('snp'), may hold values from -480 to 32224, as said below
- heritability: float32 [64], P('ind'), may hold values from 0.2 to 0.6
- genotypes: bfloat16 [8192, 32768], P('ind', 'snp'), may hold values from 0 to 2, as said below
Outputs:
- weights: float32 [64, 32768], P('ind', 'snp')
- scores: float32 [64, 8192], P(None, ('ind', 'snp'))
The draws below stay inside these ranges and needn't reach their ends.
Inputs may be any that keep to these rules, and one draw needn't show every extreme that they name: ld_band is a symmetric matrix R in band form: entry k of row i is R[i, band_start[i // 128] + k]; R[i, i] = 1; R[i, j] = 0 when |i - j| > 416 or j lies outside the SNPs; the off-diagonal magnitudes of a row sum to 2.5 at most. `band_start`: block b's window starts at 128 * b - 416 - k with k from 0 to 64; the first block has k = 64 and the last block k = 0. `genotypes`: dosages are 0, 1 or 2.
All inputs are finite; a program needn't handle non-finite values.
Results may differ from the reference program's by a relative error of at most 0.0021.
Values may be sent and summed in bfloat16 or wider, within the bound.
A program may use at most 64 MiB of HBM per device.

```python
import math
import jax
import jax.numpy as jnp
from jax import lax

TRAITS = 64
BW = 1024
BLK = 128
ITERS = 2
M_GENOME = 1100000
N_GWAS = 1000000
IND_DEV = 1024
REACH = 416
M = 32768
IND = 8192


def window_starts(key):
    block_count = M // BLK
    slack_cols = BW - BLK - 2 * REACH
    sub_key = jax.random.fold_in(key, 11)
    key_offsets, key_pick = jax.random.split(sub_key)
    offsets = jax.random.randint(key_offsets, (block_count,), 0, slack_cols + 1)
    chosen = jax.random.permutation(key_pick, block_count)
    offsets = offsets.at[chosen[0]].set(0).at[chosen[1]].set(slack_cols)
    offsets = offsets.at[0].set(slack_cols).at[block_count - 1].set(0)
    return (jnp.arange(block_count, dtype=jnp.int32) * BLK - REACH - offsets).astype(jnp.int32)


def draw_band_start(key, part):
    return window_starts(key)


def draw_ld_band(key, part):
    starts = window_starts(key)
    table_key = jax.random.fold_in(key, 23)
    table = jax.random.uniform(table_key, (M, REACH + 1), jnp.float32, 0.5, 1.0)
    reach_float = float(REACH)
    distances = jnp.arange(1, REACH + 1, dtype=jnp.float32)
    scale = 1.25 / jnp.sum(1.0 / (1.0 + distances / reach_float))
    row_ids = jnp.arange(M, dtype=jnp.int32)[:, None]
    col_ids = jnp.repeat(starts, BLK)[:, None] + jnp.arange(BW, dtype=jnp.int32)[None, :]
    gap = jnp.abs(row_ids - col_ids)
    anchor = jnp.clip(jnp.minimum(row_ids, col_ids), 0, M - 1)
    picked = table[anchor, jnp.clip(gap, 0, REACH)]
    entries = scale * picked / (1.0 + gap.astype(jnp.float32) / reach_float)
    inside = (gap <= REACH) & (col_ids >= 0) & (col_ids < M)
    return jnp.where(gap == 0, 1.0, jnp.where(inside, entries, 0.0)).astype(jnp.float32)


def draw_beta_hat(key, part):
    sub_key = jax.random.fold_in(key, 53)
    keys = jax.random.split(sub_key, 6)
    positions = jnp.arange(M, dtype=jnp.float32)
    wave_lengths = 4.0 * REACH * jnp.exp(jax.random.uniform(keys[0], (TRAITS, 6), jnp.float32, 0.0, math.log(8.0)))
    angular = 2.0 * math.pi / wave_lengths
    phases = jax.random.uniform(keys[1], (TRAITS, 6), jnp.float32, 0.0, 2.0 * math.pi)
    coefs = 0.5 * jax.random.normal(keys[2], (TRAITS, 6), jnp.float32)
    smooth = jnp.zeros((TRAITS, M), jnp.float32)
    for term in range(6):
        smooth = smooth + coefs[:, term:term + 1] * jnp.cos(positions[None, :] * angular[:, term:term + 1] + phases[:, term:term + 1])
    region_count = M // BW + 1
    region_amp = jnp.exp(jax.random.uniform(keys[3], (TRAITS, region_count), jnp.float32, math.log(0.2), math.log(2.5)))
    trait_amp = jnp.exp(jax.random.uniform(keys[4], (TRAITS, 1), jnp.float32, math.log(0.3), math.log(1.5)))
    region_index = jnp.arange(M, dtype=jnp.int32) // BW
    envelope = trait_amp * jnp.take(region_amp, region_index, axis=1)
    noise = jax.random.normal(keys[5], (TRAITS, M), jnp.float32)
    return jnp.clip(envelope * smooth + noise, -8.0, 8.0).astype(jnp.float32)


def draw_genotypes(key, part):
    sub_key = jax.random.fold_in(key, 37)
    base_key, dose_key = jax.random.split(sub_key)
    base = jax.random.uniform(base_key, (M,), jnp.float32, 0.04, 0.12)

    def row_block(block_index):
        rows_key = jax.random.fold_in(dose_key, block_index)
        uniforms = jax.random.uniform(rows_key, (2, IND_DEV, M), jnp.float32)
        person = (block_index * IND_DEV + jnp.arange(IND_DEV)).astype(jnp.float32)
        chance = base[None, :] * (1.0 + 3.0 * person / IND)[:, None]
        return jnp.sum((uniforms < chance[None]).astype(jnp.float32), axis=0).astype(jnp.bfloat16)
    blocks = lax.map(row_block, jnp.arange(IND // IND_DEV))
    return blocks.reshape(IND, M)


def steps_of(own_key, shape, pieces, least, high):
    level, own = 1.0, jax.random.fold_in(own_key, 6)
    for axis_at, blocks in pieces:
        heights = jnp.exp(jax.random.uniform(jax.random.fold_in(own, axis_at), (blocks,), jnp.float32, least / len(pieces), high / len(pieces)))
        level = level * jnp.repeat(heights, shape[axis_at] // blocks).reshape([-1 if axis == axis_at else 1 for axis in range(len(shape))])
    return level


def setup_inputs(seed: int = 0) -> dict:
    arg_keys = jax.random.split(jax.random.key(seed), 6)
    beta_hat = draw_beta_hat(jax.random.fold_in(arg_keys[5], 71), 0)
    ld_band = draw_ld_band(jax.random.fold_in(arg_keys[5], 71), 0)
    band_start = draw_band_start(jax.random.fold_in(arg_keys[5], 71), 0)
    heritability = jnp.clip(jnp.exp(math.log(0.6) - 1.0986123 * jax.random.uniform(arg_keys[3], (TRAITS,), jnp.float32) ** steps_of(arg_keys[3], (TRAITS,), ((0, 8),), -0.2, 0.2)), 0.2, 0.6)
    genotypes = draw_genotypes(jax.random.fold_in(arg_keys[5], 71), 0)
    return {"beta_hat": beta_hat, "ld_band": ld_band, "band_start": band_start, "heritability": heritability, "genotypes": genotypes}


def apply_operator(vector, ld_band, band_start, ridge_shift):
    halo_cols = BW - BLK
    padded = jnp.pad(vector, ((0, 0), (halo_cols, halo_cols)))
    blocks = ld_band.reshape(M // BLK, BLK, BW)

    def one_block(pair_item):
        first_col, band_rows = pair_item
        window = lax.dynamic_slice_in_dim(padded, (first_col + halo_cols).astype(jnp.int32), BW, 1)
        return jnp.dot(window, band_rows.T, precision=lax.Precision.HIGHEST)
    block_out = lax.map(one_block, (band_start, blocks))
    product = jnp.transpose(block_out, (1, 0, 2)).reshape(vector.shape[0], M)
    return product + ridge_shift[:, None] * vector

def reference(beta_hat, ld_band, band_start, heritability, genotypes):
    ridge_shift = M_GENOME / N_GWAS / heritability
    weights = jnp.zeros_like(beta_hat)
    residual = beta_hat
    direction = beta_hat
    norm_now = lax.optimization_barrier(jnp.sum(residual * residual, axis=1))
    for turn_index in range(ITERS):
        product = apply_operator(direction, ld_band, band_start, ridge_shift)
        step_size = norm_now / lax.optimization_barrier(jnp.sum(direction * product, axis=1))
        weights = weights + step_size[:, None] * direction
        residual = residual - step_size[:, None] * product
        if turn_index + 1 < ITERS:
            norm_next = lax.optimization_barrier(jnp.sum(residual * residual, axis=1))
            direction = residual + (norm_next / norm_now)[:, None] * direction
            norm_now = norm_next
    rounded = weights.astype(jnp.bfloat16)
    raw_scores = lax.dot_general(rounded, genotypes, (((1,), (1,)), ((), ())), preferred_element_type=jnp.float32)
    average = lax.optimization_barrier(jnp.sum(raw_scores, axis=1)) / raw_scores.shape[1]
    centred = raw_scores - average[:, None]
    variance = lax.optimization_barrier(jnp.sum(centred * centred, axis=1)) / raw_scores.shape[1]
    scores = centred * lax.rsqrt(variance + 1e-05)[:, None]
    return (weights, scores)
```

```python
import functools

import jax
import jax.numpy as jnp
from jax import lax
from jax.experimental import pallas as pl
from jax.experimental.pallas import tpu as pltpu
from jax.sharding import PartitionSpec as P

BLK = 128
M_GENOME = 1100000
N_GWAS = 1000000
SNP, IND = 32, 8
Y, Z, X = 4, 8, 4
NB = 8
TR = 8
COLS = NB * BLK
HALO = 512
SPAN = 1152
SHARE = 32
MESH = pl.DeviceIdType.MESH
NT = (((1,), (1,)), ((), ()))
F32, BF16 = jnp.float32, jnp.bfloat16


def ring(n):
    return sorted(range(n), key=lambda k: -min(k, n - k))


SNP_OFFSETS = sorted(
    ((a, b) for a in range(Y) for b in range(Z) if (a, b) != (0, 0)),
    key=lambda q: -(min(q[0], Y - q[0]) + min(q[1], Z - q[1])),
)
IND_OFFSETS = [(a, c) for a in ring(X) for c in (1, 0) if (a, c) != (0, 0)]


def split(value):
    high = value.astype(BF16).astype(F32)
    return jnp.concatenate([high, value - high], axis=0).astype(BF16)


def fold(out):
    return out[0:8, 0:BLK] + out[8:16, 0:BLK] + out[0:8, BLK:] + out[8:16, BLK:]


def local_part(vec, hilo, acc):
    for b in range(NB):
        own0, own1 = max(0, BLK * b - HALO), min(COLS, BLK * b + SPAN - HALO)
        k0 = own0 + HALO - BLK * b
        out = lax.dot_general(
            vec[:, own0:own1], hilo[b, :, k0 : k0 + own1 - own0], NT, preferred_element_type=F32
        )
        acc[:, b * BLK : (b + 1) * BLK] = fold(out)


def halo_part(left, right, hilo, acc):
    for b in range(NB):
        if b < 4:
            vec, k0, k1 = left[:, BLK * b :], 0, HALO - BLK * b
        else:
            vec, k0, k1 = right[:, : BLK * (b - 3)], HALO + COLS - BLK * b, SPAN
        out = lax.dot_general(vec, hilo[b, :, k0:k1], NT, preferred_element_type=F32)
        acc[:, b * BLK : (b + 1) * BLK] += fold(out)


def wait_for(ref, sem):
    pltpu.make_async_copy(ref, ref, sem).wait()


def lane_sum(value):
    return jnp.sum(value, axis=1, keepdims=True)


def kernel(
    start_ref,
    herit_ref,
    beta_ref,
    ld_ref,
    geno_ref,
    weights_ref,
    scores_ref,
    ldbuf,
    hilo,
    geno,
    acc,
    ubuf,
    halo,
    mom_own,
    mom_in,
    wall,
    part,
    part_in,
    stat_own,
    stat_in,
    stat_own2,
    stat_in2,
    ld_sem,
    geno_sem,
    halo_send,
    halo_recv,
    send_sem,
    recv_sem,
):
    s, i = lax.axis_index("snp"), lax.axis_index("ind")
    y, z, x, core = s // Z, s % Z, i // 2, i % 2

    def snp_peer(dy, dz):
        return lax.rem(y + dy, Y) * Z + lax.rem(z + dz, Z)

    def ind_peer(dx, dc):
        return lax.rem(x + dx, X) * 2 + lax.rem(core + dc, 2)

    def load(b):
        return pltpu.make_async_copy(ld_ref.at[pl.ds(b * BLK, BLK)], ldbuf.at[b], ld_sem.at[b])

    for b in range(NB):
        load(b).start()
    load_geno = pltpu.make_async_copy(geno_ref, geno, geno_sem)
    load_geno.start()

    barrier = pltpu.get_barrier_semaphore()
    for dy, dz in SNP_OFFSETS:
        pl.semaphore_signal(barrier, inc=1, device_id=(snp_peer(dy, dz), i), device_id_type=MESH)
    for dx, dc in IND_OFFSETS:
        pl.semaphore_signal(barrier, inc=1, device_id=(s, ind_peer(dx, dc)), device_id_type=MESH)
    pl.semaphore_wait(barrier, len(SNP_OFFSETS) + len(IND_OFFSETS))

    right, left = lax.rem(s + 1, SNP), lax.rem(s + SNP - 1, SNP)

    def send_halo(src, turn):
        copies = [
            pltpu.make_async_remote_copy(
                src_ref=src.at[:, COLS - HALO :],
                dst_ref=halo.at[turn, 0],
                send_sem=halo_send.at[turn, 0],
                recv_sem=halo_recv.at[turn, 0],
                device_id=(right, i),
                device_id_type=MESH,
            ),
            pltpu.make_async_remote_copy(
                src_ref=src.at[:, :HALO],
                dst_ref=halo.at[turn, 1],
                send_sem=halo_send.at[turn, 1],
                recv_sem=halo_recv.at[turn, 1],
                device_id=(left, i),
                device_id_type=MESH,
            ),
        ]
        for copy in copies:
            copy.start()
        return copies

    halo0 = send_halo(beta_ref, 0)

    for b in range(NB):
        load(b).wait()
        shift = start_ref[b] - (BLK * (s * NB + b) - HALO)

        def rows(k, carry, b=b, shift=shift):
            r0 = pl.multiple_of(k * 32, 32)
            value = ldbuf[b, pl.ds(r0, 32), :]
            value = jnp.concatenate([value, jnp.zeros((32, SPAN - COLS), F32)], axis=1)
            value = pltpu.roll(value, shift, 1)
            high = value.astype(BF16)
            hilo[b, pl.ds(r0, 32), :] = high
            hilo[b, pl.ds(BLK + r0, 32), :] = (value - high.astype(F32)).astype(BF16)
            return carry

        lax.fori_loop(0, BLK // 32, rows, 0)

    def off_diagonal(value, turn, copies):
        parts = split(value)
        local_part(parts, hilo, acc)
        for copy in copies:
            copy.wait_recv()
        halo_part(split(halo[turn, 0]), split(halo[turn, 1]), hilo, acc)
        return acc[...] - (parts[0:8].astype(F32) + parts[8:16].astype(F32))

    beta = beta_ref[...]
    u = off_diagonal(beta, 0, halo0)
    ubuf[...] = u
    halo1 = send_halo(ubuf, 1)

    p0 = lane_sum(beta * beta)
    p1 = lane_sum(beta * u)
    theta = jnp.where(p0 > 0, p1 / p0, 0.0)
    e = u - theta * beta
    q = lane_sum(e * e)
    t = lane_sum(e * beta)
    g = off_diagonal(u, 1, halo1) - theta * u
    f = lane_sum(e * g)
    h = lane_sum(beta * g)

    lane = lax.broadcasted_iota(jnp.int32, (TR, BLK), 1)
    tile = jnp.broadcast_to(p0, (TR, BLK))
    for k, value in enumerate((theta, q, t, f, h)):
        tile = jnp.where(lane >= 16 * (k + 1), value, tile)
    mom_own[...] = tile
    mom_in[len(SNP_OFFSETS)] = tile
    for j, (dy, dz) in enumerate(SNP_OFFSETS):
        pltpu.make_async_remote_copy(
            src_ref=mom_own,
            dst_ref=mom_in.at[j],
            send_sem=send_sem.at[0],
            recv_sem=recv_sem.at[0],
            device_id=(snp_peer(dy, dz), i),
            device_id_type=MESH,
        ).start()

    row = lax.broadcasted_iota(jnp.int32, (TR, 1), 0)
    herit = jnp.zeros((TR, 1), F32)
    for k in range(TR):
        herit = jnp.where(row == k, herit_ref[k], herit)
    kappa = 1.0 + (M_GENOME / N_GWAS) / herit

    wait_for(mom_in.at[0 : len(SNP_OFFSETS)], recv_sem.at[0])
    p0_d, th_d, q_d, t_d, f_d, h_d = [mom_in[:, :, 16 * k : 16 * k + 1] for k in range(6)]
    p0 = jnp.sum(p0_d, axis=0)
    theta = jnp.sum(p0_d * th_d + t_d, axis=0) / p0
    delta = th_d - theta[None]
    q = jnp.sum(q_d + delta * (2.0 * t_d + delta * p0_d), axis=0)
    t = jnp.sum(t_d + delta * p0_d, axis=0)
    f = jnp.sum(
        f_d + delta * (q_d + th_d * t_d + h_d + delta * (t_d + th_d * p0_d)), axis=0
    )
    a11 = p0 * (theta + kappa)
    a12 = q + (theta + kappa) * t
    a22 = f + kappa * q
    det = a11 * a22 - a12 * a12
    c1 = jnp.where(det > 0, (t * a11 - p0 * a12) / det, 0.0)
    c0 = (p0 - c1 * a12) / a11
    weights = (c0 - c1 * theta) * beta + c1 * u
    weights_ref[...] = weights

    wall[i] = jnp.concatenate([weights[:, 0:HALO], weights[:, HALO:]], axis=0).astype(BF16)
    for dx, dc in IND_OFFSETS:
        pltpu.make_async_remote_copy(
            src_ref=wall.at[i],
            dst_ref=wall.at[i],
            send_sem=send_sem.at[1],
            recv_sem=recv_sem.at[1],
            device_id=(s, ind_peer(dx, dc)),
            device_id_type=MESH,
        ).start()
    load_geno.wait()
    wait_for(wall.at[0 : len(IND_OFFSETS)], recv_sem.at[1])
    every = wall[...].astype(F32)
    rounded = jnp.concatenate(
        [every[:, 0:8].reshape(64, HALO), every[:, 8:16].reshape(64, HALO)], axis=1
    ).astype(BF16)

    slot = {offset: j for j, offset in enumerate(SNP_OFFSETS)}
    for dy in ring(Y):
        group = lax.rem(y + dy, Y)
        rows = geno[pl.ds(pl.multiple_of(group * 256, 256), 256), :]
        out = lax.dot_general(rows, rounded, NT, preferred_element_type=F32).reshape(Z, 2, 16, 64)
        part[pl.ds(group * Z, Z)] = jnp.concatenate([out[:, 0], out[:, 1]], axis=2)
        for dz in ring(Z):
            if (dy, dz) != (0, 0):
                peer = group * Z + lax.rem(z + dz, Z)
                pltpu.make_async_remote_copy(
                    src_ref=part.at[peer],
                    dst_ref=part_in.at[slot[dy, dz]],
                    send_sem=send_sem.at[2],
                    recv_sem=recv_sem.at[2],
                    device_id=(peer, i),
                    device_id_type=MESH,
                ).start()
    own = part[s]
    wait_for(part_in, recv_sem.at[2])
    raw = own + jnp.sum(part_in[...], axis=0)

    half = lax.broadcasted_iota(jnp.int32, (1, BLK), 1) < 64

    def both(value):
        return value + pltpu.roll(value, 64, 1)

    mean = both(jnp.sum(raw, axis=0, keepdims=True)) * (1.0 / SHARE)
    spread = both(jnp.sum((raw - mean) * (raw - mean), axis=0, keepdims=True))
    stat = jnp.where(half, mean, spread)

    def merge(values, count, size):
        total = jnp.sum(values, axis=0)
        mean = total * (1.0 / count)
        apart = jnp.where(half, values - mean, 0.0)
        squares = jnp.sum(apart * apart, axis=0) * float(size)
        return jnp.where(half, mean, total + pltpu.roll(squares, 64, 1))

    stat_own[...] = stat
    stat_in[len(SNP_OFFSETS)] = stat
    for j, (dy, dz) in enumerate(SNP_OFFSETS):
        pltpu.make_async_remote_copy(
            src_ref=stat_own,
            dst_ref=stat_in.at[j],
            send_sem=send_sem.at[3],
            recv_sem=recv_sem.at[3],
            device_id=(snp_peer(dy, dz), i),
            device_id_type=MESH,
        ).start()
    wait_for(stat_in.at[0 : len(SNP_OFFSETS)], recv_sem.at[3])
    stat = merge(stat_in[...], SNP, SHARE)
    stat_own2[...] = stat
    stat_in2[len(IND_OFFSETS)] = stat
    for j, (dx, dc) in enumerate(IND_OFFSETS):
        pltpu.make_async_remote_copy(
            src_ref=stat_own2,
            dst_ref=stat_in2.at[j],
            send_sem=send_sem.at[4],
            recv_sem=recv_sem.at[4],
            device_id=(s, ind_peer(dx, dc)),
            device_id_type=MESH,
        ).start()
    wait_for(stat_in2.at[0 : len(IND_OFFSETS)], recv_sem.at[4])
    stat = merge(stat_in2[...], IND, SHARE * SNP)
    swapped = pltpu.roll(stat, 64, 1)
    mean = jnp.where(half, stat, swapped)
    variance = jnp.where(half, swapped, stat) * (1.0 / (SHARE * SNP * IND))
    scores = (raw - mean) * lax.rsqrt(variance + 1e-05)
    scores_ref[0:16, :] = scores[:, 0:64]
    scores_ref[16:32, :] = scores[:, 64:128]

    for copy in halo0 + halo1:
        copy.wait_send()
    wait_for(mom_in.at[0 : len(SNP_OFFSETS)], send_sem.at[0])
    wait_for(wall.at[0 : len(IND_OFFSETS)], send_sem.at[1])
    wait_for(part_in, send_sem.at[2])
    wait_for(stat_in.at[0 : len(SNP_OFFSETS)], send_sem.at[3])
    wait_for(stat_in2.at[0 : len(IND_OFFSETS)], send_sem.at[4])


def local(beta_hat, ld_band, band_start, heritability, genotypes):
    vmem, smem = pl.BlockSpec(memory_space=pltpu.VMEM), pl.BlockSpec(memory_space=pltpu.SMEM)
    anywhere = pl.BlockSpec(memory_space=pl.ANY)
    dma = pltpu.SemaphoreType.DMA
    weights, scores = pl.pallas_call(
        kernel,
        out_shape=(
            jax.ShapeDtypeStruct((TR, COLS), F32),
            jax.ShapeDtypeStruct((SHARE, 64), F32),
        ),
        in_specs=[smem, smem, vmem, anywhere, anywhere],
        out_specs=(vmem, vmem),
        scratch_shapes=[
            pltpu.VMEM((NB, BLK, COLS), F32),
            pltpu.VMEM((NB, 2 * BLK, SPAN), BF16),
            pltpu.VMEM((1024, COLS), BF16),
            pltpu.VMEM((TR, COLS), F32),
            pltpu.VMEM((TR, COLS), F32),
            pltpu.VMEM((2, 2, TR, HALO), F32),
            pltpu.VMEM((TR, BLK), F32),
            pltpu.VMEM((SNP, TR, BLK), F32),
            pltpu.VMEM((IND, 16, HALO), BF16),
            pltpu.VMEM((SNP, 16, BLK), F32),
            pltpu.VMEM((SNP - 1, 16, BLK), F32),
            pltpu.VMEM((1, BLK), F32),
            pltpu.VMEM((SNP, 1, BLK), F32),
            pltpu.VMEM((1, BLK), F32),
            pltpu.VMEM((IND, 1, BLK), F32),
            dma((NB,)),
            dma,
            dma((2, 2)),
            dma((2, 2)),
            dma((5,)),
            dma((5,)),
        ],
        name="ldpred_scores",
        compiler_params=pltpu.CompilerParams(
            collective_id=0, has_side_effects=True, vmem_limit_bytes=40 << 20
        ),
    )(band_start, heritability, beta_hat, ld_band, genotypes)
    return weights, scores.T


def solution(mesh):
    placed = (P("ind", "snp"), P("snp", None), P("snp"), P("ind"), P("ind", "snp"))
    return jax.shard_map(
        local,
        mesh=mesh,
        in_specs=placed,
        out_specs=(P("ind", "snp"), P(None, ("ind", "snp"))),
        check_vma=False,
    )
```

```python
import functools

import jax
import jax.numpy as jnp
from jax import lax
from jax.experimental import pallas as pl
from jax.experimental.pallas import tpu as pltpu
from jax.sharding import PartitionSpec as P

BLK = 128
M_GENOME = 1100000
N_GWAS = 1000000
SNP, IND = 32, 8
Y, Z, X = 4, 8, 4
NB = 8
TR = 8
COLS = NB * BLK
HALO = 512
SPAN = 1152
SHARE = 32
MESH = pl.DeviceIdType.MESH
NT = (((1,), (1,)), ((), ()))
F32, BF16 = jnp.float32, jnp.bfloat16


def ring(n):
    return sorted(range(n), key=lambda k: -min(k, n - k))


SNP_OFFSETS = sorted(
    ((a, b) for a in range(Y) for b in range(Z) if (a, b) != (0, 0)),
    key=lambda q: -(min(q[0], Y - q[0]) + min(q[1], Z - q[1])),
)
IND_OFFSETS = [(a, c) for a in ring(X) for c in (1, 0) if (a, c) != (0, 0)]


def split(value):
    high = value.astype(BF16).astype(F32)
    return jnp.concatenate([high, value - high], axis=0).astype(BF16)


def fold(out):
    return out[0:8, 0:BLK] + out[8:16, 0:BLK] + out[0:8, BLK:] + out[8:16, BLK:]


def local_part(vec, hilo, acc):
    for b in range(NB):
        own0, own1 = max(0, BLK * b - HALO), min(COLS, BLK * b + SPAN - HALO)
        k0 = own0 + HALO - BLK * b
        out = lax.dot_general(
            vec[:, own0:own1], hilo[b, :, k0 : k0 + own1 - own0], NT, preferred_element_type=F32
        )
        acc[:, b * BLK : (b + 1) * BLK] = fold(out)


def halo_part(left, right, hilo, acc):
    for b in range(NB):
        if b < 4:
            vec, k0, k1 = left[:, BLK * b :], 0, HALO - BLK * b
        else:
            vec, k0, k1 = right[:, : BLK * (b - 3)], HALO + COLS - BLK * b, SPAN
        out = lax.dot_general(vec, hilo[b, :, k0:k1], NT, preferred_element_type=F32)
        acc[:, b * BLK : (b + 1) * BLK] += fold(out)


def wait_for(ref, sem):
    pltpu.make_async_copy(ref, ref, sem).wait()


def lane_sum(value):
    return jnp.sum(value, axis=1, keepdims=True)


def kernel(
    start_hbm,
    herit_hbm,
    beta_hbm,
    ld_ref,
    geno_ref,
    weights_ref,
    scores_ref,
    start_ref,
    herit_ref,
    beta_ref,
    ldbuf,
    hilo,
    geno,
    acc,
    ubuf,
    halo,
    mom_own,
    mom_in,
    wall,
    part,
    part_in,
    stat_own,
    stat_in,
    stat_own2,
    stat_in2,
    ld_sem,
    geno_sem,
    small_sem,
    halo_send,
    halo_recv,
    send_sem,
    recv_sem,
):
    s, i = lax.axis_index("snp"), lax.axis_index("ind")
    y, z, x, core = s // Z, s % Z, i // 2, i % 2

    def snp_peer(dy, dz):
        return lax.rem(y + dy, Y) * Z + lax.rem(z + dz, Z)

    def ind_peer(dx, dc):
        return lax.rem(x + dx, X) * 2 + lax.rem(core + dc, 2)

    def load(b):
        return pltpu.make_async_copy(ld_ref.at[pl.ds(b * BLK, BLK)], ldbuf.at[b], ld_sem.at[b])

    small = [
        pltpu.make_async_copy(src, dst, small_sem.at[k])
        for k, (src, dst) in enumerate(
            ((beta_hbm, beta_ref), (start_hbm, start_ref), (herit_hbm, herit_ref))
        )
    ]
    for copy in small:
        copy.start()
    for b in range(NB):
        load(b).start()
    load_geno = pltpu.make_async_copy(geno_ref, geno, geno_sem)
    load_geno.start()

    barrier = pltpu.get_barrier_semaphore()
    for dy, dz in SNP_OFFSETS:
        pl.semaphore_signal(barrier, inc=1, device_id=(snp_peer(dy, dz), i), device_id_type=MESH)
    for dx, dc in IND_OFFSETS:
        pl.semaphore_signal(barrier, inc=1, device_id=(s, ind_peer(dx, dc)), device_id_type=MESH)
    pl.semaphore_wait(barrier, len(SNP_OFFSETS) + len(IND_OFFSETS))

    for copy in small:
        copy.wait()
    right, left = lax.rem(s + 1, SNP), lax.rem(s + SNP - 1, SNP)

    def send_halo(src, turn):
        copies = [
            pltpu.make_async_remote_copy(
                src_ref=src.at[:, COLS - HALO :],
                dst_ref=halo.at[turn, 0],
                send_sem=halo_send.at[turn, 0],
                recv_sem=halo_recv.at[turn, 0],
                device_id=(right, i),
                device_id_type=MESH,
            ),
            pltpu.make_async_remote_copy(
                src_ref=src.at[:, :HALO],
                dst_ref=halo.at[turn, 1],
                send_sem=halo_send.at[turn, 1],
                recv_sem=halo_recv.at[turn, 1],
                device_id=(left, i),
                device_id_type=MESH,
            ),
        ]
        for copy in copies:
            copy.start()
        return copies

    halo0 = send_halo(beta_ref, 0)

    for b in range(NB):
        load(b).wait()
        shift = start_ref[b] - (BLK * (s * NB + b) - HALO)

        def rows(k, carry, b=b, shift=shift):
            r0 = pl.multiple_of(k * 32, 32)
            value = ldbuf[b, pl.ds(r0, 32), :]
            value = jnp.concatenate([value, jnp.zeros((32, SPAN - COLS), F32)], axis=1)
            value = pltpu.roll(value, shift, 1)
            high = value.astype(BF16)
            hilo[b, pl.ds(r0, 32), :] = high
            hilo[b, pl.ds(BLK + r0, 32), :] = (value - high.astype(F32)).astype(BF16)
            return carry

        lax.fori_loop(0, BLK // 32, rows, 0)

    def off_diagonal(value, turn, copies):
        parts = split(value)
        local_part(parts, hilo, acc)
        for copy in copies:
            copy.wait_recv()
        halo_part(split(halo[turn, 0]), split(halo[turn, 1]), hilo, acc)
        return acc[...] - (parts[0:8].astype(F32) + parts[8:16].astype(F32))

    beta = beta_ref[...]
    u = off_diagonal(beta, 0, halo0)
    ubuf[...] = u
    halo1 = send_halo(ubuf, 1)

    p0 = lane_sum(beta * beta)
    p1 = lane_sum(beta * u)
    theta = jnp.where(p0 > 0, p1 / p0, 0.0)
    e = u - theta * beta
    q = lane_sum(e * e)
    t = lane_sum(e * beta)
    g = off_diagonal(u, 1, halo1) - theta * u
    f = lane_sum(e * g)
    h = lane_sum(beta * g)

    lane = lax.broadcasted_iota(jnp.int32, (TR, BLK), 1)
    tile = jnp.broadcast_to(p0, (TR, BLK))
    for k, value in enumerate((theta, q, t, f, h)):
        tile = jnp.where(lane >= 16 * (k + 1), value, tile)
    mom_own[...] = tile
    mom_in[len(SNP_OFFSETS)] = tile
    for j, (dy, dz) in enumerate(SNP_OFFSETS):
        pltpu.make_async_remote_copy(
            src_ref=mom_own,
            dst_ref=mom_in.at[j],
            send_sem=send_sem.at[0],
            recv_sem=recv_sem.at[0],
            device_id=(snp_peer(dy, dz), i),
            device_id_type=MESH,
        ).start()

    row = lax.broadcasted_iota(jnp.int32, (TR, 1), 0)
    herit = jnp.zeros((TR, 1), F32)
    for k in range(TR):
        herit = jnp.where(row == k, herit_ref[k], herit)
    kappa = 1.0 + (M_GENOME / N_GWAS) / herit

    wait_for(mom_in.at[0 : len(SNP_OFFSETS)], recv_sem.at[0])
    p0_d, th_d, q_d, t_d, f_d, h_d = [mom_in[:, :, 16 * k : 16 * k + 1] for k in range(6)]
    p0 = jnp.sum(p0_d, axis=0)
    theta = jnp.sum(p0_d * th_d + t_d, axis=0) / p0
    delta = th_d - theta[None]
    q = jnp.sum(q_d + delta * (2.0 * t_d + delta * p0_d), axis=0)
    t = jnp.sum(t_d + delta * p0_d, axis=0)
    f = jnp.sum(
        f_d + delta * (q_d + th_d * t_d + h_d + delta * (t_d + th_d * p0_d)), axis=0
    )
    a11 = p0 * (theta + kappa)
    a12 = q + (theta + kappa) * t
    a22 = f + kappa * q
    det = a11 * a22 - a12 * a12
    c1 = jnp.where(det > 0, (t * a11 - p0 * a12) / det, 0.0)
    c0 = (p0 - c1 * a12) / a11
    weights = (c0 - c1 * theta) * beta + c1 * u
    weights_ref[...] = weights

    wall[i] = jnp.concatenate([weights[:, 0:HALO], weights[:, HALO:]], axis=0).astype(BF16)
    for dx, dc in IND_OFFSETS:
        pltpu.make_async_remote_copy(
            src_ref=wall.at[i],
            dst_ref=wall.at[i],
            send_sem=send_sem.at[1],
            recv_sem=recv_sem.at[1],
            device_id=(s, ind_peer(dx, dc)),
            device_id_type=MESH,
        ).start()
    load_geno.wait()
    wait_for(wall.at[0 : len(IND_OFFSETS)], recv_sem.at[1])
    every = wall[...].astype(F32)
    rounded = jnp.concatenate(
        [every[:, 0:8].reshape(64, HALO), every[:, 8:16].reshape(64, HALO)], axis=1
    ).astype(BF16)

    slot = {offset: j for j, offset in enumerate(SNP_OFFSETS)}
    for dy in ring(Y):
        group = lax.rem(y + dy, Y)
        rows = geno[pl.ds(pl.multiple_of(group * 256, 256), 256), :]
        out = lax.dot_general(rows, rounded, NT, preferred_element_type=F32).reshape(Z, 2, 16, 64)
        part[pl.ds(group * Z, Z)] = jnp.concatenate([out[:, 0], out[:, 1]], axis=2)
        for dz in ring(Z):
            if (dy, dz) != (0, 0):
                peer = group * Z + lax.rem(z + dz, Z)
                pltpu.make_async_remote_copy(
                    src_ref=part.at[peer],
                    dst_ref=part_in.at[slot[dy, dz]],
                    send_sem=send_sem.at[2],
                    recv_sem=recv_sem.at[2],
                    device_id=(peer, i),
                    device_id_type=MESH,
                ).start()
    own = part[s]
    wait_for(part_in, recv_sem.at[2])
    raw = own + jnp.sum(part_in[...], axis=0)

    half = lax.broadcasted_iota(jnp.int32, (1, BLK), 1) < 64

    def both(value):
        return value + pltpu.roll(value, 64, 1)

    mean = both(jnp.sum(raw, axis=0, keepdims=True)) * (1.0 / SHARE)
    spread = both(jnp.sum((raw - mean) * (raw - mean), axis=0, keepdims=True))
    stat = jnp.where(half, mean, spread)

    def merge(values, count, size):
        total = jnp.sum(values, axis=0)
        mean = total * (1.0 / count)
        apart = jnp.where(half, values - mean, 0.0)
        squares = jnp.sum(apart * apart, axis=0) * float(size)
        return jnp.where(half, mean, total + pltpu.roll(squares, 64, 1))

    stat_own[...] = stat
    stat_in[len(SNP_OFFSETS)] = stat
    for j, (dy, dz) in enumerate(SNP_OFFSETS):
        pltpu.make_async_remote_copy(
            src_ref=stat_own,
            dst_ref=stat_in.at[j],
            send_sem=send_sem.at[3],
            recv_sem=recv_sem.at[3],
            device_id=(snp_peer(dy, dz), i),
            device_id_type=MESH,
        ).start()
    wait_for(stat_in.at[0 : len(SNP_OFFSETS)], recv_sem.at[3])
    stat = merge(stat_in[...], SNP, SHARE)
    stat_own2[...] = stat
    stat_in2[len(IND_OFFSETS)] = stat
    for j, (dx, dc) in enumerate(IND_OFFSETS):
        pltpu.make_async_remote_copy(
            src_ref=stat_own2,
            dst_ref=stat_in2.at[j],
            send_sem=send_sem.at[4],
            recv_sem=recv_sem.at[4],
            device_id=(s, ind_peer(dx, dc)),
            device_id_type=MESH,
        ).start()
    wait_for(stat_in2.at[0 : len(IND_OFFSETS)], recv_sem.at[4])
    stat = merge(stat_in2[...], IND, SHARE * SNP)
    swapped = pltpu.roll(stat, 64, 1)
    mean = jnp.where(half, stat, swapped)
    variance = jnp.where(half, swapped, stat) * (1.0 / (SHARE * SNP * IND))
    scores = (raw - mean) * lax.rsqrt(variance + 1e-05)
    scores_ref[0:16, :] = scores[:, 0:64]
    scores_ref[16:32, :] = scores[:, 64:128]

    for copy in halo0 + halo1:
        copy.wait_send()
    wait_for(mom_in.at[0 : len(SNP_OFFSETS)], send_sem.at[0])
    wait_for(wall.at[0 : len(IND_OFFSETS)], send_sem.at[1])
    wait_for(part_in, send_sem.at[2])
    wait_for(stat_in.at[0 : len(SNP_OFFSETS)], send_sem.at[3])
    wait_for(stat_in2.at[0 : len(IND_OFFSETS)], send_sem.at[4])


def local(beta_hat, ld_band, band_start, heritability, genotypes):
    vmem, anywhere = pl.BlockSpec(memory_space=pltpu.VMEM), pl.BlockSpec(memory_space=pl.ANY)
    dma = pltpu.SemaphoreType.DMA
    weights, scores = pl.pallas_call(
        kernel,
        out_shape=(
            jax.ShapeDtypeStruct((TR, COLS), F32),
            jax.ShapeDtypeStruct((SHARE, 64), F32),
        ),
        in_specs=[anywhere] * 5,
        out_specs=(vmem, vmem),
        scratch_shapes=[
            pltpu.SMEM((NB,), jnp.int32),
            pltpu.SMEM((TR,), F32),
            pltpu.VMEM((TR, COLS), F32),
            pltpu.VMEM((NB, BLK, COLS), F32),
            pltpu.VMEM((NB, 2 * BLK, SPAN), BF16),
            pltpu.VMEM((1024, COLS), BF16),
            pltpu.VMEM((TR, COLS), F32),
            pltpu.VMEM((TR, COLS), F32),
            pltpu.VMEM((2, 2, TR, HALO), F32),
            pltpu.VMEM((TR, BLK), F32),
            pltpu.VMEM((SNP, TR, BLK), F32),
            pltpu.VMEM((IND, 16, HALO), BF16),
            pltpu.VMEM((SNP, 16, BLK), F32),
            pltpu.VMEM((SNP - 1, 16, BLK), F32),
            pltpu.VMEM((1, BLK), F32),
            pltpu.VMEM((SNP, 1, BLK), F32),
            pltpu.VMEM((1, BLK), F32),
            pltpu.VMEM((IND, 1, BLK), F32),
            dma((NB,)),
            dma,
            dma((3,)),
            dma((2, 2)),
            dma((2, 2)),
            dma((5,)),
            dma((5,)),
        ],
        name="ldpred_scores",
        compiler_params=pltpu.CompilerParams(
            collective_id=0, has_side_effects=True, vmem_limit_bytes=60 << 20
        ),
    )(band_start, heritability, beta_hat, ld_band, genotypes)
    return weights, scores.T


def solution(mesh):
    placed = (P("ind", "snp"), P("snp", None), P("snp"), P("ind"), P("ind", "snp"))
    return jax.shard_map(
        local,
        mesh=mesh,
        in_specs=placed,
        out_specs=(P("ind", "snp"), P(None, ("ind", "snp"))),
        check_vma=False,
    )
```

```python
import functools

import jax
import jax.numpy as jnp
from jax import lax
from jax.experimental import pallas as pl
from jax.experimental.pallas import tpu as pltpu
from jax.sharding import PartitionSpec as P

BLK = 128
M_GENOME = 1100000
N_GWAS = 1000000
SNP, IND = 32, 8
Y, Z, X = 4, 8, 4
NB = 8
TR = 8
COLS = NB * BLK
HALO = 512
SPAN = 1152
SHARE = 32
MESH = pl.DeviceIdType.MESH
NT = (((1,), (1,)), ((), ()))
F32, BF16 = jnp.float32, jnp.bfloat16


def ring(n):
    return sorted(range(n), key=lambda k: -min(k, n - k))


SNP_OFFSETS = sorted(
    ((a, b) for a in range(Y) for b in range(Z) if (a, b) != (0, 0)),
    key=lambda q: -(min(q[0], Y - q[0]) + min(q[1], Z - q[1])),
)
IND_OFFSETS = [(a, c) for a in ring(X) for c in (1, 0) if (a, c) != (0, 0)]


def split(value):
    high = value.astype(BF16).astype(F32)
    return jnp.concatenate([high, value - high], axis=0).astype(BF16)


def fold(out):
    return out[0:8, 0:BLK] + out[8:16, 0:BLK] + out[0:8, BLK:] + out[8:16, BLK:]


def local_part(vec, hilo, acc):
    for b in range(NB):
        own0, own1 = max(0, BLK * b - HALO), min(COLS, BLK * b + SPAN - HALO)
        k0 = own0 + HALO - BLK * b
        out = lax.dot_general(
            vec[:, own0:own1], hilo[b, :, k0 : k0 + own1 - own0], NT, preferred_element_type=F32
        )
        acc[:, b * BLK : (b + 1) * BLK] = fold(out)


def halo_part(left, right, hilo, acc):
    for b in range(NB):
        if b < 4:
            vec, k0, k1 = left[:, BLK * b :], 0, HALO - BLK * b
        else:
            vec, k0, k1 = right[:, : BLK * (b - 3)], HALO + COLS - BLK * b, SPAN
        out = lax.dot_general(vec, hilo[b, :, k0:k1], NT, preferred_element_type=F32)
        acc[:, b * BLK : (b + 1) * BLK] += fold(out)


def wait_for(ref, sem):
    pltpu.make_async_copy(ref, ref, sem).wait()


def lane_sum(value):
    return jnp.sum(value, axis=1, keepdims=True)


def kernel(
    start_hbm,
    herit_hbm,
    beta_hbm,
    ld_ref,
    geno_ref,
    weights_out,
    scores_out,
    start_ref,
    herit_ref,
    beta_ref,
    ldbuf,
    hilo,
    geno,
    acc,
    ubuf,
    halo,
    basis,
    mom_own,
    mom_in,
    coef_own,
    coef_in,
    part,
    part_in,
    stat_own,
    stat_in,
    weights_ref,
    scores_ref,
    ld_sem,
    geno_sem,
    small_sem,
    out_sem,
    halo_send,
    halo_recv,
    send_sem,
    recv_sem,
):
    s, i = lax.axis_index("snp"), lax.axis_index("ind")
    y, z, x, core = s // Z, s % Z, i // 2, i % 2

    def snp_peer(dy, dz):
        return lax.rem(y + dy, Y) * Z + lax.rem(z + dz, Z)

    def ind_peer(dx, dc):
        return lax.rem(x + dx, X) * 2 + lax.rem(core + dc, 2)

    near_peers = [
        (y * Z + lax.rem(z + dz, Z), x * 2 + lax.rem(core + dc, 2))
        for dz in ring(Z)
        for dc in (1, 0)
        if (dz, dc) != (0, 0)
    ]
    far_peers = [
        (lax.rem(y + dy, Y) * Z + z, lax.rem(x + dx, X) * 2 + core)
        for dx in ring(X)
        for dy in ring(Y)
        if (dx, dy) != (0, 0)
    ]

    def load(b):
        return pltpu.make_async_copy(ld_ref.at[pl.ds(b * BLK, BLK)], ldbuf.at[b], ld_sem.at[b])

    small = [
        pltpu.make_async_copy(src, dst, small_sem.at[k])
        for k, (src, dst) in enumerate(
            ((beta_hbm, beta_ref), (start_hbm, start_ref), (herit_hbm, herit_ref))
        )
    ]
    for copy in small:
        copy.start()
    for b in range(NB):
        load(b).start()
    load_geno = pltpu.make_async_copy(geno_ref, geno, geno_sem)
    load_geno.start()

    barrier = pltpu.get_barrier_semaphore()
    for dy, dz in SNP_OFFSETS:
        pl.semaphore_signal(barrier, inc=1, device_id=(snp_peer(dy, dz), i), device_id_type=MESH)
    for dx, dc in IND_OFFSETS:
        pl.semaphore_signal(barrier, inc=1, device_id=(s, ind_peer(dx, dc)), device_id_type=MESH)
    pl.semaphore_wait(barrier, len(SNP_OFFSETS) + len(IND_OFFSETS))

    for copy in small:
        copy.wait()
    right, left = lax.rem(s + 1, SNP), lax.rem(s + SNP - 1, SNP)

    def send_halo(src, turn):
        copies = [
            pltpu.make_async_remote_copy(
                src_ref=src.at[:, COLS - HALO :],
                dst_ref=halo.at[turn, 0],
                send_sem=halo_send.at[turn, 0],
                recv_sem=halo_recv.at[turn, 0],
                device_id=(right, i),
                device_id_type=MESH,
            ),
            pltpu.make_async_remote_copy(
                src_ref=src.at[:, :HALO],
                dst_ref=halo.at[turn, 1],
                send_sem=halo_send.at[turn, 1],
                recv_sem=halo_recv.at[turn, 1],
                device_id=(left, i),
                device_id_type=MESH,
            ),
        ]
        for copy in copies:
            copy.start()
        return copies

    halo0 = send_halo(beta_ref, 0)
    beta = beta_ref[...]

    def gather(turn, parts):
        basis[turn, i] = parts
        for dx, dc in IND_OFFSETS:
            pltpu.make_async_remote_copy(
                src_ref=basis.at[turn, i],
                dst_ref=basis.at[turn, i],
                send_sem=send_sem.at[turn],
                recv_sem=recv_sem.at[turn],
                device_id=(s, ind_peer(dx, dc)),
                device_id_type=MESH,
            ).start()

    beta_parts = split(beta)
    gather(0, beta_parts)

    for b in range(NB):
        load(b).wait()
        shift = start_ref[b] - (BLK * (s * NB + b) - HALO)

        def rows(k, carry, b=b, shift=shift):
            r0 = pl.multiple_of(k * 32, 32)
            value = ldbuf[b, pl.ds(r0, 32), :]
            value = jnp.concatenate([value, jnp.zeros((32, SPAN - COLS), F32)], axis=1)
            value = pltpu.roll(value, shift, 1)
            high = value.astype(BF16)
            hilo[b, pl.ds(r0, 32), :] = high
            hilo[b, pl.ds(BLK + r0, 32), :] = (value - high.astype(F32)).astype(BF16)
            return carry

        lax.fori_loop(0, BLK // 32, rows, 0)

    def off_diagonal(parts, turn, copies):
        for copy in copies:
            copy.wait_recv()
        halo_part(split(halo[turn, 0]), split(halo[turn, 1]), hilo, acc)
        return acc[...] - (parts[0:8].astype(F32) + parts[8:16].astype(F32))

    local_part(beta_parts, hilo, acc)
    u = off_diagonal(beta_parts, 0, halo0)
    u_parts = split(u)
    gather(1, u_parts)
    ubuf[...] = u
    halo1 = send_halo(ubuf, 1)

    local_part(u_parts, hilo, acc)
    p0 = lane_sum(beta * beta)
    p1 = lane_sum(beta * u)
    theta = jnp.where(p0 > 0, p1 / p0, 0.0)
    e = u - theta * beta
    q = lane_sum(e * e)
    t = lane_sum(e * beta)

    slot = {offset: j for j, offset in enumerate(SNP_OFFSETS)}
    lane = lax.broadcasted_iota(jnp.int32, (1, BLK), 1)
    half = lane < 64

    def both(value):
        return value + pltpu.roll(value, 64, value.ndim - 1)

    def partial_scores(turn):
        wait_for(basis.at[turn, 0 : len(IND_OFFSETS)], recv_sem.at[turn])
        every = basis[turn].astype(F32)
        every = jnp.concatenate(
            [every[:, 0:8].reshape(64, COLS), every[:, 8:16].reshape(64, COLS)], axis=0
        ).astype(BF16)
        for dy in ring(Y):
            group = lax.rem(y + dy, Y)
            rows = geno[pl.ds(pl.multiple_of(group * 256, 256), 256), :]
            out = both(lax.dot_general(rows, every, NT, preferred_element_type=F32))
            out = out.reshape(Z, 2, 16, BLK)
            part[turn, pl.ds(group * Z, Z)] = jnp.where(half, out[:, 0], out[:, 1])
            for dz in ring(Z):
                if (dy, dz) != (0, 0):
                    peer = group * Z + lax.rem(z + dz, Z)
                    pltpu.make_async_remote_copy(
                        src_ref=part.at[turn, peer],
                        dst_ref=part_in.at[turn, slot[dy, dz]],
                        send_sem=send_sem.at[2 + turn],
                        recv_sem=recv_sem.at[2 + turn],
                        device_id=(peer, i),
                        device_id_type=MESH,
                    ).start()

    def total_scores(turn):
        own = part[turn, s]
        wait_for(part_in.at[turn], recv_sem.at[2 + turn])
        return own + jnp.sum(part_in[turn], axis=0)

    load_geno.wait()
    partial_scores(0)

    g = off_diagonal(u_parts, 1, halo1) - theta * u
    f = lane_sum(e * g)
    h = lane_sum(beta * g)
    tile_lane = lax.broadcasted_iota(jnp.int32, (TR, BLK), 1)
    tile_row = lax.broadcasted_iota(jnp.int32, (TR, BLK), 0)
    tile = jnp.broadcast_to(p0, (TR, BLK))
    for k, value in enumerate((theta, q, t, f, h)):
        tile = jnp.where(tile_lane >= 16 * (k + 1), value, tile)
    tile = jnp.where(tile_lane % 16 == tile_row, tile, 0.0)
    sums = jnp.sum(tile, axis=0, keepdims=True)
    mom_own[...] = sums
    mom_in[len(SNP_OFFSETS)] = sums
    for j, (dy, dz) in enumerate(SNP_OFFSETS):
        pltpu.make_async_remote_copy(
            src_ref=mom_own,
            dst_ref=mom_in.at[j],
            send_sem=send_sem.at[4],
            recv_sem=recv_sem.at[4],
            device_id=(snp_peer(dy, dz), i),
            device_id_type=MESH,
        ).start()

    partial_scores(1)

    herit = jnp.ones((1, BLK), F32)
    for k in range(TR):
        herit = jnp.where(lane == k, herit_ref[k], herit)
    kappa = 1.0 + (M_GENOME / N_GWAS) / herit

    wait_for(mom_in.at[0 : len(SNP_OFFSETS)], recv_sem.at[4])
    moments = mom_in[...]
    p0_d, th_d, q_d, t_d, f_d, h_d = [
        moments if k == 0 else pltpu.roll(moments, BLK - 16 * k, 2) for k in range(6)
    ]
    p0 = jnp.sum(p0_d, axis=0)
    theta = jnp.sum(p0_d * th_d + t_d, axis=0) / p0
    delta = th_d - theta[None]
    q = jnp.sum(q_d + delta * (2.0 * t_d + delta * p0_d), axis=0)
    t = jnp.sum(t_d + delta * p0_d, axis=0)
    f = jnp.sum(
        f_d + delta * (q_d + th_d * t_d + h_d + delta * (t_d + th_d * p0_d)), axis=0
    )
    a11 = p0 * (theta + kappa)
    a12 = q + (theta + kappa) * t
    a22 = f + kappa * q
    det = a11 * a22 - a12 * a12
    c1 = jnp.where(det > 0, (t * a11 - p0 * a12) / det, 0.0)
    c0 = (p0 - c1 * a12) / a11 - c1 * theta

    own_lanes = lane < TR
    coef = jnp.where(own_lanes, c0, 0.0) + pltpu.roll(jnp.where(own_lanes, c1, 0.0), 64, 1)
    coef = pltpu.roll(coef, i * TR, 1)
    coef_own[...] = coef
    coef_in[len(IND_OFFSETS)] = coef
    for j, (dx, dc) in enumerate(IND_OFFSETS):
        pltpu.make_async_remote_copy(
            src_ref=coef_own,
            dst_ref=coef_in.at[j],
            send_sem=send_sem.at[5],
            recv_sem=recv_sem.at[5],
            device_id=(s, ind_peer(dx, dc)),
            device_id_type=MESH,
        ).start()

    diagonal = tile_lane == tile_row
    c0 = lane_sum(jnp.where(diagonal, c0, 0.0))
    c1 = lane_sum(jnp.where(diagonal, c1, 0.0))
    weights_ref[...] = c0 * beta + c1 * u
    store_weights = pltpu.make_async_copy(weights_ref, weights_out, out_sem.at[0])
    store_weights.start()

    beta_scores = total_scores(0)
    wait_for(coef_in.at[0 : len(IND_OFFSETS)], recv_sem.at[5])
    coef = jnp.sum(coef_in[...], axis=0)
    swapped = pltpu.roll(coef, 64, 1)
    beta_scores = beta_scores * jnp.where(half, coef, swapped)
    raw = beta_scores + total_scores(1) * jnp.where(half, swapped, coef)

    mean = both(jnp.sum(raw, axis=0, keepdims=True)) * (1.0 / SHARE)
    spread = both(jnp.sum((raw - mean) * (raw - mean), axis=0, keepdims=True))
    stat = jnp.where(half, mean, spread)
    size = SHARE
    for turn, peers in enumerate((near_peers, far_peers)):
        stat_own[turn] = stat
        stat_in[turn, len(peers)] = stat
        for j, peer in enumerate(peers):
            pltpu.make_async_remote_copy(
                src_ref=stat_own.at[turn],
                dst_ref=stat_in.at[turn, j],
                send_sem=send_sem.at[6 + turn],
                recv_sem=recv_sem.at[6 + turn],
                device_id=peer,
                device_id_type=MESH,
            ).start()
        wait_for(stat_in.at[turn, 0 : len(peers)], recv_sem.at[6 + turn])
        count = len(peers) + 1
        values = stat_in[turn]
        total = jnp.sum(values, axis=0)
        mean = total * (1.0 / count)
        apart = jnp.where(half, values - mean, 0.0)
        squares = jnp.sum(apart * apart, axis=0) * float(size)
        stat = jnp.where(half, mean, total + pltpu.roll(squares, 64, 1))
        size *= count
    swapped = pltpu.roll(stat, 64, 1)
    mean = jnp.where(half, stat, swapped)
    variance = jnp.where(half, swapped, stat) * (1.0 / size)
    scores = (raw - mean) * lax.rsqrt(variance + 1e-05)
    scores_ref[0:16, :] = scores[:, 0:64]
    scores_ref[16:32, :] = scores[:, 64:128]
    store_scores = pltpu.make_async_copy(scores_ref, scores_out, out_sem.at[1])
    store_scores.start()

    for copy in halo0 + halo1:
        copy.wait_send()
    for turn in range(2):
        wait_for(basis.at[turn, 0 : len(IND_OFFSETS)], send_sem.at[turn])
        wait_for(part_in.at[turn], send_sem.at[2 + turn])
        wait_for(stat_in.at[turn, 0:15], send_sem.at[6 + turn])
    wait_for(mom_in.at[0 : len(SNP_OFFSETS)], send_sem.at[4])
    wait_for(coef_in.at[0 : len(IND_OFFSETS)], send_sem.at[5])
    store_weights.wait()
    store_scores.wait()


def hand_over(weights_ref, scores_ref, weights_out, scores_out, sem):
    copies = [
        pltpu.make_async_copy(weights_ref, weights_out, sem.at[0]),
        pltpu.make_async_copy(scores_ref, scores_out, sem.at[1]),
    ]
    for copy in copies:
        copy.start()
    for copy in copies:
        copy.wait()


def local(beta_hat, ld_band, band_start, heritability, genotypes):
    anywhere = pl.BlockSpec(memory_space=pl.ANY)
    dma = pltpu.SemaphoreType.DMA
    weights, scores = pl.pallas_call(
        kernel,
        out_shape=(
            jax.ShapeDtypeStruct((TR, COLS), F32),
            jax.ShapeDtypeStruct((SHARE, 64), F32),
        ),
        in_specs=[anywhere] * 5,
        out_specs=(anywhere, anywhere),
        scratch_shapes=[
            pltpu.SMEM((NB,), jnp.int32),
            pltpu.SMEM((TR,), F32),
            pltpu.VMEM((TR, COLS), F32),
            pltpu.VMEM((NB, BLK, COLS), F32),
            pltpu.VMEM((NB, 2 * BLK, SPAN), BF16),
            pltpu.VMEM((1024, COLS), BF16),
            pltpu.VMEM((TR, COLS), F32),
            pltpu.VMEM((TR, COLS), F32),
            pltpu.VMEM((2, 2, TR, HALO), F32),
            pltpu.VMEM((2, IND, 16, COLS), BF16),
            pltpu.VMEM((1, BLK), F32),
            pltpu.VMEM((SNP, 1, BLK), F32),
            pltpu.VMEM((1, BLK), F32),
            pltpu.VMEM((IND, 1, BLK), F32),
            pltpu.VMEM((2, SNP, 16, BLK), F32),
            pltpu.VMEM((2, SNP - 1, 16, BLK), F32),
            pltpu.VMEM((2, 1, BLK), F32),
            pltpu.VMEM((2, 16, 1, BLK), F32),
            pltpu.VMEM((TR, COLS), F32),
            pltpu.VMEM((SHARE, 64), F32),
            dma((NB,)),
            dma,
            dma((3,)),
            dma((2,)),
            dma((2, 2)),
            dma((2, 2)),
            dma((8,)),
            dma((8,)),
        ],
        name="ldpred_scores",
        compiler_params=pltpu.CompilerParams(
            collective_id=0, has_side_effects=True, vmem_limit_bytes=60 << 20
        ),
    )(band_start, heritability, beta_hat, ld_band, genotypes)
    weights, scores = pl.pallas_call(
        hand_over,
        out_shape=(
            jax.ShapeDtypeStruct((TR, COLS), F32),
            jax.ShapeDtypeStruct((SHARE, 64), F32),
        ),
        in_specs=[anywhere] * 2,
        out_specs=(anywhere, anywhere),
        scratch_shapes=[dma((2,))],
        name="hand_over",
        compiler_params=pltpu.CompilerParams(vmem_limit_bytes=60 << 20),
    )(weights, scores)
    return weights, scores.T


def solution(mesh):
    placed = (P("ind", "snp"), P("snp", None), P("snp"), P("ind"), P("ind", "snp"))
    return jax.shard_map(
        local,
        mesh=mesh,
        in_specs=placed,
        out_specs=(P("ind", "snp"), P(None, ("ind", "snp"))),
        check_vma=False,
    )
```

```python
import functools

import jax
import jax.numpy as jnp
from jax import lax
from jax.experimental import pallas as pl
from jax.experimental.pallas import tpu as pltpu
from jax.sharding import PartitionSpec as P

BLK = 128
M_GENOME = 1100000
N_GWAS = 1000000
SNP, IND = 32, 8
Y, Z, X = 4, 8, 4
NB = 8
TR = 8
COLS = NB * BLK
HALO = 512
SPAN = 1152
SHARE = 32
MESH = pl.DeviceIdType.MESH
NT = (((1,), (1,)), ((), ()))
F32, BF16 = jnp.float32, jnp.bfloat16


def ring(n):
    return sorted(range(n), key=lambda k: -min(k, n - k))


SNP_OFFSETS = sorted(
    ((a, b) for a in range(Y) for b in range(Z) if (a, b) != (0, 0)),
    key=lambda q: -(min(q[0], Y - q[0]) + min(q[1], Z - q[1])),
)
CHIP_OFFSETS = sorted(
    ((a, b, c) for a in range(X) for b in range(Y) for c in range(Z) if (a, b, c) != (0, 0, 0)),
    key=lambda q: -(min(q[0], X - q[0]) + min(q[1], Y - q[1]) + min(q[2], Z - q[2])),
)
IND_OFFSETS = [(a, c) for a in ring(X) for c in (1, 0) if (a, c) != (0, 0)]


def split(value):
    high = value.astype(BF16).astype(F32)
    return jnp.concatenate([high, value - high], axis=0).astype(BF16)


def fold(out):
    return out[0:8, 0:BLK] + out[8:16, 0:BLK] + out[0:8, BLK:] + out[8:16, BLK:]


def local_part(vec, hilo, acc):
    for b in range(NB):
        own0, own1 = max(0, BLK * b - HALO), min(COLS, BLK * b + SPAN - HALO)
        k0 = own0 + HALO - BLK * b
        out = lax.dot_general(
            vec[:, own0:own1], hilo[b, :, k0 : k0 + own1 - own0], NT, preferred_element_type=F32
        )
        acc[:, b * BLK : (b + 1) * BLK] = fold(out)


def halo_part(left, right, hilo, acc):
    for b in range(NB):
        if b < 4:
            vec, k0, k1 = left[:, BLK * b :], 0, HALO - BLK * b
        else:
            vec, k0, k1 = right[:, : BLK * (b - 3)], HALO + COLS - BLK * b, SPAN
        out = lax.dot_general(vec, hilo[b, :, k0:k1], NT, preferred_element_type=F32)
        acc[:, b * BLK : (b + 1) * BLK] += fold(out)


def wait_for(ref, sem):
    pltpu.make_async_copy(ref, ref, sem).wait()


def lane_sum(value):
    return jnp.sum(value, axis=1, keepdims=True)


def kernel(
    start_hbm,
    herit_hbm,
    beta_hbm,
    ld_ref,
    geno_ref,
    weights_out,
    scores_out,
    start_ref,
    herit_ref,
    beta_ref,
    ldbuf,
    hilo,
    geno,
    acc,
    ubuf,
    halo,
    basis,
    mom_own,
    mom_in,
    coef_own,
    coef_in,
    part,
    part_in,
    lines_in,
    line_own,
    line_in,
    stat_own,
    stat_in,
    weights_ref,
    scores_ref,
    ld_sem,
    geno_sem,
    small_sem,
    out_sem,
    halo_send,
    halo_recv,
    send_sem,
    recv_sem,
):
    s, i = lax.axis_index("snp"), lax.axis_index("ind")
    y, z, x, core = s // Z, s % Z, i // 2, i % 2

    def snp_peer(dy, dz):
        return lax.rem(y + dy, Y) * Z + lax.rem(z + dz, Z)

    def ind_peer(dx, dc):
        return lax.rem(x + dx, X) * 2 + lax.rem(core + dc, 2)

    near_peers = [(s, i + 1 - 2 * core)]
    far_peers = [
        (lax.rem(y + dy, Y) * Z + lax.rem(z + dz, Z), lax.rem(x + dx, X) * 2 + core)
        for dx, dy, dz in CHIP_OFFSETS
    ]

    def load(b):
        return pltpu.make_async_copy(ld_ref.at[pl.ds(b * BLK, BLK)], ldbuf.at[b], ld_sem.at[b])

    small = [
        pltpu.make_async_copy(src, dst, small_sem.at[k])
        for k, (src, dst) in enumerate(
            ((beta_hbm, beta_ref), (start_hbm, start_ref), (herit_hbm, herit_ref))
        )
    ]
    for copy in small:
        copy.start()
    for b in range(NB):
        load(b).start()
    load_geno = pltpu.make_async_copy(geno_ref, geno, geno_sem)
    load_geno.start()

    barrier = pltpu.get_barrier_semaphore()
    for dy, dz in SNP_OFFSETS:
        pl.semaphore_signal(barrier, inc=1, device_id=(snp_peer(dy, dz), i), device_id_type=MESH)
    for dx, dc in IND_OFFSETS:
        pl.semaphore_signal(barrier, inc=1, device_id=(s, ind_peer(dx, dc)), device_id_type=MESH)
    pl.semaphore_wait(barrier, len(SNP_OFFSETS) + len(IND_OFFSETS))

    for copy in small:
        copy.wait()
    right, left = lax.rem(s + 1, SNP), lax.rem(s + SNP - 1, SNP)

    def send_halo(src, turn):
        copies = [
            pltpu.make_async_remote_copy(
                src_ref=src.at[:, COLS - HALO :],
                dst_ref=halo.at[turn, 0],
                send_sem=halo_send.at[turn, 0],
                recv_sem=halo_recv.at[turn, 0],
                device_id=(right, i),
                device_id_type=MESH,
            ),
            pltpu.make_async_remote_copy(
                src_ref=src.at[:, :HALO],
                dst_ref=halo.at[turn, 1],
                send_sem=halo_send.at[turn, 1],
                recv_sem=halo_recv.at[turn, 1],
                device_id=(left, i),
                device_id_type=MESH,
            ),
        ]
        for copy in copies:
            copy.start()
            pending.append(copy.wait_send)
        return copies

    pending = []
    halo0 = send_halo(beta_ref, 0)
    beta = beta_ref[...]

    def gather(turn, parts):
        basis[turn, i] = parts
        for dx, dc in IND_OFFSETS:
            pltpu.make_async_remote_copy(
                src_ref=basis.at[turn, i],
                dst_ref=basis.at[turn, i],
                send_sem=send_sem.at[turn],
                recv_sem=recv_sem.at[turn],
                device_id=(s, ind_peer(dx, dc)),
                device_id_type=MESH,
            ).start()
        pending.append(lambda: wait_for(basis.at[turn, 0 : len(IND_OFFSETS)], send_sem.at[turn]))

    beta_parts = split(beta)
    gather(0, beta_parts)

    for b in range(NB):
        load(b).wait()
        shift = start_ref[b] - (BLK * (s * NB + b) - HALO)

        def rows(k, carry, b=b, shift=shift):
            r0 = pl.multiple_of(k * 32, 32)
            value = ldbuf[b, pl.ds(r0, 32), :]
            value = jnp.concatenate([value, jnp.zeros((32, SPAN - COLS), F32)], axis=1)
            value = pltpu.roll(value, shift, 1)
            high = value.astype(BF16)
            hilo[b, pl.ds(r0, 32), :] = high
            hilo[b, pl.ds(BLK + r0, 32), :] = (value - high.astype(F32)).astype(BF16)
            return carry

        lax.fori_loop(0, BLK // 32, rows, 0)

    def off_diagonal(parts, turn, copies):
        for copy in copies:
            copy.wait_recv()
        halo_part(split(halo[turn, 0]), split(halo[turn, 1]), hilo, acc)
        return acc[...] - (parts[0:8].astype(F32) + parts[8:16].astype(F32))

    local_part(beta_parts, hilo, acc)
    u = off_diagonal(beta_parts, 0, halo0)
    u_parts = split(u)
    gather(1, u_parts)
    ubuf[...] = u
    halo1 = send_halo(ubuf, 1)

    local_part(u_parts, hilo, acc)
    p0 = lane_sum(beta * beta)
    p1 = lane_sum(beta * u)
    theta = jnp.where(p0 > 0, p1 / p0, 0.0)
    e = u - theta * beta
    q = lane_sum(e * e)
    t = lane_sum(e * beta)

    slot = {offset: j for j, offset in enumerate(SNP_OFFSETS)}
    lane = lax.broadcasted_iota(jnp.int32, (1, BLK), 1)
    half = lane < 64

    def both(value):
        return value + pltpu.roll(value, 64, value.ndim - 1)

    def partial_scores(turn):
        wait_for(basis.at[turn, 0 : len(IND_OFFSETS)], recv_sem.at[turn])
        every = basis[turn].astype(F32)
        every = jnp.concatenate(
            [every[:, 0:8].reshape(64, COLS), every[:, 8:16].reshape(64, COLS)], axis=0
        ).astype(BF16)
        for dy in ring(Y):
            group = lax.rem(y + dy, Y)
            rows = geno[pl.ds(pl.multiple_of(group * 256, 256), 256), :]
            out = both(lax.dot_general(rows, every, NT, preferred_element_type=F32))
            out = out.reshape(Z, 2, 16, BLK)
            part[turn, pl.ds(group * Z, Z)] = jnp.where(half, out[:, 0], out[:, 1])
            if turn == 0:
                if dy:
                    along_y(dy)
                continue
            for dz in ring(Z):
                if (dy, dz) != (0, 0):
                    peer = group * Z + lax.rem(z + dz, Z)
                    pltpu.make_async_remote_copy(
                        src_ref=part.at[turn, peer],
                        dst_ref=part_in.at[slot[dy, dz]],
                        send_sem=send_sem.at[3],
                        recv_sem=recv_sem.at[3],
                        device_id=(peer, i),
                        device_id_type=MESH,
                    ).start()
        if turn == 1:
            pending.append(lambda: wait_for(part_in, send_sem.at[3]))

    def along_y(dy):
        group = lax.rem(y + dy, Y)
        pltpu.make_async_remote_copy(
            src_ref=part.at[0, pl.ds(group * Z, Z)],
            dst_ref=lines_in.at[dy - 1],
            send_sem=send_sem.at[2],
            recv_sem=recv_sem.at[2],
            device_id=(group * Z + z, i),
            device_id_type=MESH,
        ).start()

    def along_z():
        wait_for(lines_in, recv_sem.at[2])
        line_own[...] = part[0, pl.ds(y * Z, Z)] + jnp.sum(lines_in[...], axis=0)
        for dz in ring(Z)[:-1]:
            peer = lax.rem(z + dz, Z)
            pltpu.make_async_remote_copy(
                src_ref=line_own.at[peer],
                dst_ref=line_in.at[dz - 1],
                send_sem=send_sem.at[8],
                recv_sem=recv_sem.at[8],
                device_id=(y * Z + peer, i),
                device_id_type=MESH,
            ).start()
        pending.append(lambda: wait_for(lines_in, send_sem.at[2]))
        pending.append(lambda: wait_for(line_in, send_sem.at[8]))

    def total_scores(turn):
        if turn == 0:
            wait_for(line_in, recv_sem.at[8])
            return line_own[z] + jnp.sum(line_in[...], axis=0)
        wait_for(part_in, recv_sem.at[3])
        return part[1, s] + jnp.sum(part_in[...], axis=0)

    load_geno.wait()
    partial_scores(0)

    g = off_diagonal(u_parts, 1, halo1) - theta * u
    f = lane_sum(e * g)
    h = lane_sum(beta * g)
    tile_lane = lax.broadcasted_iota(jnp.int32, (TR, BLK), 1)
    tile_row = lax.broadcasted_iota(jnp.int32, (TR, BLK), 0)
    tile = jnp.broadcast_to(p0, (TR, BLK))
    for k, value in enumerate((theta, q, t, f, h)):
        tile = jnp.where(tile_lane >= 16 * (k + 1), value, tile)
    tile = jnp.where(tile_lane % 16 == tile_row, tile, 0.0)
    sums = jnp.sum(tile, axis=0, keepdims=True)
    mom_own[...] = sums
    mom_in[len(SNP_OFFSETS)] = sums
    for j, (dy, dz) in enumerate(SNP_OFFSETS):
        pltpu.make_async_remote_copy(
            src_ref=mom_own,
            dst_ref=mom_in.at[j],
            send_sem=send_sem.at[4],
            recv_sem=recv_sem.at[4],
            device_id=(snp_peer(dy, dz), i),
            device_id_type=MESH,
        ).start()

    pending.append(lambda: wait_for(mom_in.at[0 : len(SNP_OFFSETS)], send_sem.at[4]))

    partial_scores(1)
    along_z()

    herit = jnp.ones((1, BLK), F32)
    for k in range(TR):
        herit = jnp.where(lane == k, herit_ref[k], herit)
    kappa = 1.0 + (M_GENOME / N_GWAS) / herit

    wait_for(mom_in.at[0 : len(SNP_OFFSETS)], recv_sem.at[4])
    moments = mom_in[...]
    p0_d, th_d, q_d, t_d, f_d, h_d = [
        moments if k == 0 else pltpu.roll(moments, BLK - 16 * k, 2) for k in range(6)
    ]
    p0 = jnp.sum(p0_d, axis=0)
    theta = jnp.sum(p0_d * th_d + t_d, axis=0) / p0
    delta = th_d - theta[None]
    q = jnp.sum(q_d + delta * (2.0 * t_d + delta * p0_d), axis=0)
    t = jnp.sum(t_d + delta * p0_d, axis=0)
    f = jnp.sum(
        f_d + delta * (q_d + th_d * t_d + h_d + delta * (t_d + th_d * p0_d)), axis=0
    )
    a11 = p0 * (theta + kappa)
    a12 = q + (theta + kappa) * t
    a22 = f + kappa * q
    det = a11 * a22 - a12 * a12
    c1 = jnp.where(det > 0, (t * a11 - p0 * a12) / det, 0.0)
    c0 = (p0 - c1 * a12) / a11 - c1 * theta

    own_lanes = lane < TR
    coef = jnp.where(own_lanes, c0, 0.0) + pltpu.roll(jnp.where(own_lanes, c1, 0.0), 64, 1)
    coef = pltpu.roll(coef, i * TR, 1)
    coef_own[...] = coef
    coef_in[len(IND_OFFSETS)] = coef
    for j, (dx, dc) in enumerate(IND_OFFSETS):
        pltpu.make_async_remote_copy(
            src_ref=coef_own,
            dst_ref=coef_in.at[j],
            send_sem=send_sem.at[5],
            recv_sem=recv_sem.at[5],
            device_id=(s, ind_peer(dx, dc)),
            device_id_type=MESH,
        ).start()

    pending.append(lambda: wait_for(coef_in.at[0 : len(IND_OFFSETS)], send_sem.at[5]))

    diagonal = tile_lane == tile_row
    c0 = lane_sum(jnp.where(diagonal, c0, 0.0))
    c1 = lane_sum(jnp.where(diagonal, c1, 0.0))
    weights_ref[...] = c0 * beta + c1 * u
    store_weights = pltpu.make_async_copy(weights_ref, weights_out, out_sem.at[0])
    store_weights.start()

    beta_scores = total_scores(0)
    wait_for(coef_in.at[0 : len(IND_OFFSETS)], recv_sem.at[5])
    coef = jnp.sum(coef_in[...], axis=0)
    swapped = pltpu.roll(coef, 64, 1)
    beta_scores = beta_scores * jnp.where(half, coef, swapped)
    raw = beta_scores + total_scores(1) * jnp.where(half, swapped, coef)

    mean = both(jnp.sum(raw, axis=0, keepdims=True)) * (1.0 / SHARE)
    spread = both(jnp.sum((raw - mean) * (raw - mean), axis=0, keepdims=True))
    stat = jnp.where(half, mean, spread)
    size = SHARE
    for turn, peers in enumerate((near_peers, far_peers)):
        count = len(peers) + 1
        stat_own[turn] = stat
        stat_in[turn, len(peers)] = stat
        for j, peer in enumerate(peers):
            pltpu.make_async_remote_copy(
                src_ref=stat_own.at[turn],
                dst_ref=stat_in.at[turn, j],
                send_sem=send_sem.at[6 + turn],
                recv_sem=recv_sem.at[6 + turn],
                device_id=peer,
                device_id_type=MESH,
            ).start()
        arrived = stat_in.at[turn, 0 : len(peers)]
        pending.append(lambda turn=turn, arrived=arrived: wait_for(arrived, send_sem.at[6 + turn]))
        wait_for(arrived, recv_sem.at[6 + turn])
        values = stat_in[turn, 0:count]
        total = jnp.sum(values, axis=0)
        mean = total * (1.0 / count)
        apart = jnp.where(half, values - mean, 0.0)
        squares = jnp.sum(apart * apart, axis=0) * float(size)
        stat = jnp.where(half, mean, total + pltpu.roll(squares, 64, 1))
        size *= count
    swapped = pltpu.roll(stat, 64, 1)
    mean = jnp.where(half, stat, swapped)
    variance = jnp.where(half, swapped, stat) * (1.0 / size)
    scores = (raw - mean) * lax.rsqrt(variance + 1e-05)
    scores_ref[0:16, :] = scores[:, 0:64]
    scores_ref[16:32, :] = scores[:, 64:128]
    store_scores = pltpu.make_async_copy(scores_ref, scores_out, out_sem.at[1])
    store_scores.start()

    for drain in pending:
        drain()
    store_weights.wait()
    store_scores.wait()


def hand_over(weights_ref, scores_ref, weights_out, scores_out):
    weights_out[...] = weights_ref[...]
    scores_out[...] = scores_ref[...]


def local(beta_hat, ld_band, band_start, heritability, genotypes):
    vmem, anywhere = pl.BlockSpec(memory_space=pltpu.VMEM), pl.BlockSpec(memory_space=pl.ANY)
    dma = pltpu.SemaphoreType.DMA
    weights, scores = pl.pallas_call(
        kernel,
        out_shape=(
            jax.ShapeDtypeStruct((TR, COLS), F32),
            jax.ShapeDtypeStruct((SHARE, 64), F32),
        ),
        in_specs=[anywhere] * 5,
        out_specs=(anywhere, anywhere),
        scratch_shapes=[
            pltpu.SMEM((NB,), jnp.int32),
            pltpu.SMEM((TR,), F32),
            pltpu.VMEM((TR, COLS), F32),
            pltpu.VMEM((NB, BLK, COLS), F32),
            pltpu.VMEM((NB, 2 * BLK, SPAN), BF16),
            pltpu.VMEM((1024, COLS), BF16),
            pltpu.VMEM((TR, COLS), F32),
            pltpu.VMEM((TR, COLS), F32),
            pltpu.VMEM((2, 2, TR, HALO), F32),
            pltpu.VMEM((2, IND, 16, COLS), BF16),
            pltpu.VMEM((1, BLK), F32),
            pltpu.VMEM((SNP, 1, BLK), F32),
            pltpu.VMEM((1, BLK), F32),
            pltpu.VMEM((IND, 1, BLK), F32),
            pltpu.VMEM((2, SNP, 16, BLK), F32),
            pltpu.VMEM((SNP - 1, 16, BLK), F32),
            pltpu.VMEM((Y - 1, Z, 16, BLK), F32),
            pltpu.VMEM((Z, 16, BLK), F32),
            pltpu.VMEM((Z - 1, 16, BLK), F32),
            pltpu.VMEM((2, 1, BLK), F32),
            pltpu.VMEM((2, X * Y * Z, 1, BLK), F32),
            pltpu.VMEM((TR, COLS), F32),
            pltpu.VMEM((SHARE, 64), F32),
            dma((NB,)),
            dma,
            dma((3,)),
            dma((2,)),
            dma((2, 2)),
            dma((2, 2)),
            dma((9,)),
            dma((9,)),
        ],
        name="ldpred_scores",
        compiler_params=pltpu.CompilerParams(
            collective_id=0, has_side_effects=True, vmem_limit_bytes=60 << 20
        ),
    )(band_start, heritability, beta_hat, ld_band, genotypes)
    weights, scores = pl.pallas_call(
        hand_over,
        out_shape=(
            jax.ShapeDtypeStruct((TR, COLS), F32),
            jax.ShapeDtypeStruct((SHARE, 64), F32),
        ),
        in_specs=[vmem] * 2,
        out_specs=(vmem, vmem),
        name="hand_over",
        compiler_params=pltpu.CompilerParams(vmem_limit_bytes=60 << 20),
    )(weights, scores)
    return weights, scores.T


def solution(mesh):
    placed = (P("ind", "snp"), P("snp", None), P("snp"), P("ind"), P("ind", "snp"))
    return jax.shard_map(
        local,
        mesh=mesh,
        in_specs=placed,
        out_specs=(P("ind", "snp"), P(None, ("ind", "snp"))),
        check_vma=False,
    )
```

```python
import functools

import jax
import jax.numpy as jnp
from jax import lax
from jax.experimental import pallas as pl
from jax.experimental.pallas import tpu as pltpu
from jax.sharding import PartitionSpec as P

BLK = 128
M_GENOME = 1100000
N_GWAS = 1000000
SNP, IND = 32, 8
Y, Z, X = 4, 8, 4
NB = 8
TR = 8
COLS = NB * BLK
HALO = 512
SHARE = 32
MESH = pl.DeviceIdType.MESH
NT = (((1,), (1,)), ((), ()))
F32, BF16 = jnp.float32, jnp.bfloat16


def ring(n):
    return sorted(range(n), key=lambda k: -min(k, n - k))


SNP_OFFSETS = sorted(
    ((a, b) for a in range(Y) for b in range(Z) if (a, b) != (0, 0)),
    key=lambda q: -(min(q[0], Y - q[0]) + min(q[1], Z - q[1])),
)
CHIP_OFFSETS = sorted(
    ((a, b, c) for a in range(X) for b in range(Y) for c in range(Z) if (a, b, c) != (0, 0, 0)),
    key=lambda q: -(min(q[0], X - q[0]) + min(q[1], Y - q[1]) + min(q[2], Z - q[2])),
)
IND_OFFSETS = [(a, c) for a in ring(X) for c in (1, 0) if (a, c) != (0, 0)]


def split(value):
    high = value.astype(BF16).astype(F32)
    return jnp.concatenate([high, value - high], axis=0).astype(BF16)


def fold(out):
    return out[0:8, 0:BLK] + out[8:16, 0:BLK] + out[0:8, BLK:] + out[8:16, BLK:]


def window(padded, first, width, shift):
    segment = padded[:, first : first + width + BLK]
    return split(pltpu.roll(segment, width + BLK - shift, 1)[:, :width])


def product(b, vec, k0, hilo):
    out = lax.dot_general(
        vec, hilo[b, :, k0 : k0 + vec.shape[1]], NT, preferred_element_type=F32
    )
    return fold(out)


def local_part(value, shifts, hilo, acc):
    empty = jnp.zeros((TR, HALO), F32)
    padded = jnp.concatenate([empty, value, empty], axis=1)
    for b in range(NB):
        k0, k1 = max(0, 384 - BLK * b), min(COLS, 1536 - BLK * b)
        vec = window(padded, BLK * b + k0, k1 - k0, shifts[b])
        acc[:, b * BLK : (b + 1) * BLK] = product(b, vec, k0, hilo)


def halo_part(left, right, shifts, hilo, acc):
    empty = jnp.zeros((TR, BLK), F32)
    left = jnp.concatenate([left, empty], axis=1)
    right = jnp.concatenate([empty, right], axis=1)
    for b in range(NB):
        if b < 4:
            k0 = 0
            vec = window(left, BLK * b, HALO - BLK * b, shifts[b])
        else:
            k0 = 1408 - BLK * b
            vec = window(right, 0, COLS - k0, shifts[b])
        acc[:, b * BLK : (b + 1) * BLK] += product(b, vec, k0, hilo)


def wait_for(ref, sem):
    pltpu.make_async_copy(ref, ref, sem).wait()


def lane_sum(value):
    return jnp.sum(value, axis=1, keepdims=True)


def kernel(
    start_hbm,
    herit_hbm,
    beta_hbm,
    ld_ref,
    geno_ref,
    weights_out,
    scores_out,
    start_ref,
    herit_ref,
    beta_ref,
    ldbuf,
    hilo,
    geno,
    acc,
    ubuf,
    halo,
    basis,
    mom_own,
    mom_in,
    coef_own,
    coef_in,
    part,
    part_in,
    lines_in,
    line_own,
    line_in,
    stat_own,
    stat_in,
    weights_ref,
    scores_ref,
    ld_sem,
    geno_sem,
    small_sem,
    out_sem,
    halo_send,
    halo_recv,
    send_sem,
    recv_sem,
):
    s, i = lax.axis_index("snp"), lax.axis_index("ind")
    y, z, x, core = s // Z, s % Z, i // 2, i % 2

    def snp_peer(dy, dz):
        return lax.rem(y + dy, Y) * Z + lax.rem(z + dz, Z)

    def ind_peer(dx, dc):
        return lax.rem(x + dx, X) * 2 + lax.rem(core + dc, 2)

    near_peers = [(s, i + 1 - 2 * core)]
    far_peers = [
        (lax.rem(y + dy, Y) * Z + lax.rem(z + dz, Z), lax.rem(x + dx, X) * 2 + core)
        for dx, dy, dz in CHIP_OFFSETS
    ]

    def load(b):
        return pltpu.make_async_copy(ld_ref.at[pl.ds(b * BLK, BLK)], ldbuf.at[b], ld_sem.at[b])

    small = [
        pltpu.make_async_copy(src, dst, small_sem.at[k])
        for k, (src, dst) in enumerate(
            ((beta_hbm, beta_ref), (start_hbm, start_ref), (herit_hbm, herit_ref))
        )
    ]
    for copy in small:
        copy.start()
    for b in range(NB):
        load(b).start()
    load_geno = pltpu.make_async_copy(geno_ref, geno, geno_sem)
    load_geno.start()

    barrier = pltpu.get_barrier_semaphore()
    for dy, dz in SNP_OFFSETS:
        pl.semaphore_signal(barrier, inc=1, device_id=(snp_peer(dy, dz), i), device_id_type=MESH)
    for dx, dc in IND_OFFSETS:
        pl.semaphore_signal(barrier, inc=1, device_id=(s, ind_peer(dx, dc)), device_id_type=MESH)
    pl.semaphore_wait(barrier, len(SNP_OFFSETS) + len(IND_OFFSETS))

    for copy in small:
        copy.wait()
    right, left = lax.rem(s + 1, SNP), lax.rem(s + SNP - 1, SNP)

    def send_halo(src, turn):
        copies = [
            pltpu.make_async_remote_copy(
                src_ref=src.at[:, COLS - HALO :],
                dst_ref=halo.at[turn, 0],
                send_sem=halo_send.at[turn, 0],
                recv_sem=halo_recv.at[turn, 0],
                device_id=(right, i),
                device_id_type=MESH,
            ),
            pltpu.make_async_remote_copy(
                src_ref=src.at[:, :HALO],
                dst_ref=halo.at[turn, 1],
                send_sem=halo_send.at[turn, 1],
                recv_sem=halo_recv.at[turn, 1],
                device_id=(left, i),
                device_id_type=MESH,
            ),
        ]
        for copy in copies:
            copy.start()
            pending.append(copy.wait_send)
        return copies

    pending = []
    halo0 = send_halo(beta_ref, 0)
    beta = beta_ref[...]

    def gather(turn, parts):
        basis[turn, i] = parts
        for dx, dc in IND_OFFSETS:
            pltpu.make_async_remote_copy(
                src_ref=basis.at[turn, i],
                dst_ref=basis.at[turn, i],
                send_sem=send_sem.at[turn],
                recv_sem=recv_sem.at[turn],
                device_id=(s, ind_peer(dx, dc)),
                device_id_type=MESH,
            ).start()
        pending.append(lambda: wait_for(basis.at[turn, 0 : len(IND_OFFSETS)], send_sem.at[turn]))

    beta_parts = split(beta)
    gather(0, beta_parts)

    shifts = [start_ref[b] - (BLK * (s * NB + b) - HALO) for b in range(NB)]
    for b in range(NB):
        load(b).wait()

        def rows(k, carry, b=b):
            r0 = pl.multiple_of(k * 32, 32)
            value = ldbuf[b, pl.ds(r0, 32), :]
            high = value.astype(BF16)
            hilo[b, pl.ds(r0, 32), :] = high
            hilo[b, pl.ds(BLK + r0, 32), :] = (value - high.astype(F32)).astype(BF16)
            return carry

        lax.fori_loop(0, BLK // 32, rows, 0)

    def off_diagonal(parts, turn, copies):
        for copy in copies:
            copy.wait_recv()
        halo_part(halo[turn, 0], halo[turn, 1], shifts, hilo, acc)
        return acc[...] - (parts[0:8].astype(F32) + parts[8:16].astype(F32))

    local_part(beta, shifts, hilo, acc)
    u = off_diagonal(beta_parts, 0, halo0)
    u_parts = split(u)
    gather(1, u_parts)
    ubuf[...] = u
    halo1 = send_halo(ubuf, 1)

    local_part(u, shifts, hilo, acc)
    p0 = lane_sum(beta * beta)
    p1 = lane_sum(beta * u)
    theta = jnp.where(p0 > 0, p1 / p0, 0.0)
    e = u - theta * beta
    q = lane_sum(e * e)
    t = lane_sum(e * beta)

    slot = {offset: j for j, offset in enumerate(SNP_OFFSETS)}
    lane = lax.broadcasted_iota(jnp.int32, (1, BLK), 1)
    half = lane < 64

    def both(value):
        return value + pltpu.roll(value, 64, value.ndim - 1)

    def partial_scores(turn):
        wait_for(basis.at[turn, 0 : len(IND_OFFSETS)], recv_sem.at[turn])
        every = basis[turn].astype(F32)
        every = jnp.concatenate(
            [every[:, 0:8].reshape(64, COLS), every[:, 8:16].reshape(64, COLS)], axis=0
        ).astype(BF16)
        for dy in ring(Y):
            group = lax.rem(y + dy, Y)
            rows = geno[pl.ds(pl.multiple_of(group * 256, 256), 256), :]
            out = both(lax.dot_general(rows, every, NT, preferred_element_type=F32))
            out = out.reshape(Z, 2, 16, BLK)
            part[turn, pl.ds(group * Z, Z)] = jnp.where(half, out[:, 0], out[:, 1])
            if turn == 0:
                if dy:
                    along_y(dy)
                continue
            for dz in ring(Z):
                if (dy, dz) != (0, 0):
                    peer = group * Z + lax.rem(z + dz, Z)
                    pltpu.make_async_remote_copy(
                        src_ref=part.at[turn, peer],
                        dst_ref=part_in.at[slot[dy, dz]],
                        send_sem=send_sem.at[3],
                        recv_sem=recv_sem.at[3],
                        device_id=(peer, i),
                        device_id_type=MESH,
                    ).start()
        if turn == 1:
            pending.append(lambda: wait_for(part_in, send_sem.at[3]))

    def along_y(dy):
        group = lax.rem(y + dy, Y)
        pltpu.make_async_remote_copy(
            src_ref=part.at[0, pl.ds(group * Z, Z)],
            dst_ref=lines_in.at[dy - 1],
            send_sem=send_sem.at[2],
            recv_sem=recv_sem.at[2],
            device_id=(group * Z + z, i),
            device_id_type=MESH,
        ).start()

    def along_z():
        wait_for(lines_in, recv_sem.at[2])
        line_own[...] = part[0, pl.ds(y * Z, Z)] + jnp.sum(lines_in[...], axis=0)
        for dz in ring(Z)[:-1]:
            peer = lax.rem(z + dz, Z)
            pltpu.make_async_remote_copy(
                src_ref=line_own.at[peer],
                dst_ref=line_in.at[dz - 1],
                send_sem=send_sem.at[8],
                recv_sem=recv_sem.at[8],
                device_id=(y * Z + peer, i),
                device_id_type=MESH,
            ).start()
        pending.append(lambda: wait_for(lines_in, send_sem.at[2]))
        pending.append(lambda: wait_for(line_in, send_sem.at[8]))

    def total_scores(turn):
        if turn == 0:
            wait_for(line_in, recv_sem.at[8])
            return line_own[z] + jnp.sum(line_in[...], axis=0)
        wait_for(part_in, recv_sem.at[3])
        return part[1, s] + jnp.sum(part_in[...], axis=0)

    load_geno.wait()
    partial_scores(0)

    g = off_diagonal(u_parts, 1, halo1) - theta * u
    f = lane_sum(e * g)
    h = lane_sum(beta * g)
    tile_lane = lax.broadcasted_iota(jnp.int32, (TR, BLK), 1)
    tile_row = lax.broadcasted_iota(jnp.int32, (TR, BLK), 0)
    tile = jnp.broadcast_to(p0, (TR, BLK))
    for k, value in enumerate((theta, q, t, f, h)):
        tile = jnp.where(tile_lane >= 16 * (k + 1), value, tile)
    tile = jnp.where(tile_lane % 16 == tile_row, tile, 0.0)
    sums = jnp.sum(tile, axis=0, keepdims=True)
    mom_own[...] = sums
    mom_in[len(SNP_OFFSETS)] = sums
    for j, (dy, dz) in enumerate(SNP_OFFSETS):
        pltpu.make_async_remote_copy(
            src_ref=mom_own,
            dst_ref=mom_in.at[j],
            send_sem=send_sem.at[4],
            recv_sem=recv_sem.at[4],
            device_id=(snp_peer(dy, dz), i),
            device_id_type=MESH,
        ).start()

    pending.append(lambda: wait_for(mom_in.at[0 : len(SNP_OFFSETS)], send_sem.at[4]))

    partial_scores(1)
    along_z()

    herit = jnp.ones((1, BLK), F32)
    for k in range(TR):
        herit = jnp.where(lane == k, herit_ref[k], herit)
    kappa = 1.0 + (M_GENOME / N_GWAS) / herit

    wait_for(mom_in.at[0 : len(SNP_OFFSETS)], recv_sem.at[4])
    moments = mom_in[...]
    p0_d, th_d, q_d, t_d, f_d, h_d = [
        moments if k == 0 else pltpu.roll(moments, BLK - 16 * k, 2) for k in range(6)
    ]
    p0 = jnp.sum(p0_d, axis=0)
    theta = jnp.sum(p0_d * th_d + t_d, axis=0) / p0
    delta = th_d - theta[None]
    q = jnp.sum(q_d + delta * (2.0 * t_d + delta * p0_d), axis=0)
    t = jnp.sum(t_d + delta * p0_d, axis=0)
    f = jnp.sum(
        f_d + delta * (q_d + th_d * t_d + h_d + delta * (t_d + th_d * p0_d)), axis=0
    )
    a11 = p0 * (theta + kappa)
    a12 = q + (theta + kappa) * t
    a22 = f + kappa * q
    det = a11 * a22 - a12 * a12
    c1 = jnp.where(det > 0, (t * a11 - p0 * a12) / det, 0.0)
    c0 = (p0 - c1 * a12) / a11 - c1 * theta

    own_lanes = lane < TR
    coef = jnp.where(own_lanes, c0, 0.0) + pltpu.roll(jnp.where(own_lanes, c1, 0.0), 64, 1)
    coef = pltpu.roll(coef, i * TR, 1)
    coef_own[...] = coef
    coef_in[len(IND_OFFSETS)] = coef
    for j, (dx, dc) in enumerate(IND_OFFSETS):
        pltpu.make_async_remote_copy(
            src_ref=coef_own,
            dst_ref=coef_in.at[j],
            send_sem=send_sem.at[5],
            recv_sem=recv_sem.at[5],
            device_id=(s, ind_peer(dx, dc)),
            device_id_type=MESH,
        ).start()

    pending.append(lambda: wait_for(coef_in.at[0 : len(IND_OFFSETS)], send_sem.at[5]))

    diagonal = tile_lane == tile_row
    c0 = lane_sum(jnp.where(diagonal, c0, 0.0))
    c1 = lane_sum(jnp.where(diagonal, c1, 0.0))
    weights_ref[...] = c0 * beta + c1 * u
    store_weights = pltpu.make_async_copy(weights_ref, weights_out, out_sem.at[0])
    store_weights.start()

    beta_scores = total_scores(0)
    wait_for(coef_in.at[0 : len(IND_OFFSETS)], recv_sem.at[5])
    coef = jnp.sum(coef_in[...], axis=0)
    swapped = pltpu.roll(coef, 64, 1)
    beta_scores = beta_scores * jnp.where(half, coef, swapped)
    raw = beta_scores + total_scores(1) * jnp.where(half, swapped, coef)

    mean = both(jnp.sum(raw, axis=0, keepdims=True)) * (1.0 / SHARE)
    spread = both(jnp.sum((raw - mean) * (raw - mean), axis=0, keepdims=True))
    stat = jnp.where(half, mean, spread)
    size = SHARE
    for turn, peers in enumerate((near_peers, far_peers)):
        count = len(peers) + 1
        stat_own[turn] = stat
        stat_in[turn, len(peers)] = stat
        for j, peer in enumerate(peers):
            pltpu.make_async_remote_copy(
                src_ref=stat_own.at[turn],
                dst_ref=stat_in.at[turn, j],
                send_sem=send_sem.at[6 + turn],
                recv_sem=recv_sem.at[6 + turn],
                device_id=peer,
                device_id_type=MESH,
            ).start()
        arrived = stat_in.at[turn, 0 : len(peers)]
        pending.append(lambda turn=turn, arrived=arrived: wait_for(arrived, send_sem.at[6 + turn]))
        wait_for(arrived, recv_sem.at[6 + turn])
        values = stat_in[turn, 0:count]
        total = jnp.sum(values, axis=0)
        mean = total * (1.0 / count)
        apart = jnp.where(half, values - mean, 0.0)
        squares = jnp.sum(apart * apart, axis=0) * float(size)
        stat = jnp.where(half, mean, total + pltpu.roll(squares, 64, 1))
        size *= count
    swapped = pltpu.roll(stat, 64, 1)
    mean = jnp.where(half, stat, swapped)
    variance = jnp.where(half, swapped, stat) * (1.0 / size)
    scores = (raw - mean) * lax.rsqrt(variance + 1e-05)
    scores_ref[0:16, :] = scores[:, 0:64]
    scores_ref[16:32, :] = scores[:, 64:128]
    store_scores = pltpu.make_async_copy(scores_ref, scores_out, out_sem.at[1])
    store_scores.start()

    for drain in pending:
        drain()
    store_weights.wait()
    store_scores.wait()


def hand_over(weights_ref, scores_ref, weights_out, scores_out):
    weights_out[...] = weights_ref[...]
    scores_out[...] = scores_ref[...]


def local(beta_hat, ld_band, band_start, heritability, genotypes):
    vmem, anywhere = pl.BlockSpec(memory_space=pltpu.VMEM), pl.BlockSpec(memory_space=pl.ANY)
    dma = pltpu.SemaphoreType.DMA
    weights, scores = pl.pallas_call(
        kernel,
        out_shape=(
            jax.ShapeDtypeStruct((TR, COLS), F32),
            jax.ShapeDtypeStruct((SHARE, 64), F32),
        ),
        in_specs=[anywhere] * 5,
        out_specs=(anywhere, anywhere),
        scratch_shapes=[
            pltpu.SMEM((NB,), jnp.int32),
            pltpu.SMEM((TR,), F32),
            pltpu.VMEM((TR, COLS), F32),
            pltpu.VMEM((NB, BLK, COLS), F32),
            pltpu.VMEM((NB, 2 * BLK, COLS), BF16),
            pltpu.VMEM((1024, COLS), BF16),
            pltpu.VMEM((TR, COLS), F32),
            pltpu.VMEM((TR, COLS), F32),
            pltpu.VMEM((2, 2, TR, HALO), F32),
            pltpu.VMEM((2, IND, 16, COLS), BF16),
            pltpu.VMEM((1, BLK), F32),
            pltpu.VMEM((SNP, 1, BLK), F32),
            pltpu.VMEM((1, BLK), F32),
            pltpu.VMEM((IND, 1, BLK), F32),
            pltpu.VMEM((2, SNP, 16, BLK), F32),
            pltpu.VMEM((SNP - 1, 16, BLK), F32),
            pltpu.VMEM((Y - 1, Z, 16, BLK), F32),
            pltpu.VMEM((Z, 16, BLK), F32),
            pltpu.VMEM((Z - 1, 16, BLK), F32),
            pltpu.VMEM((2, 1, BLK), F32),
            pltpu.VMEM((2, X * Y * Z, 1, BLK), F32),
            pltpu.VMEM((TR, COLS), F32),
            pltpu.VMEM((SHARE, 64), F32),
            dma((NB,)),
            dma,
            dma((3,)),
            dma((2,)),
            dma((2, 2)),
            dma((2, 2)),
            dma((9,)),
            dma((9,)),
        ],
        name="ldpred_scores",
        compiler_params=pltpu.CompilerParams(
            collective_id=0, has_side_effects=True, vmem_limit_bytes=60 << 20
        ),
    )(band_start, heritability, beta_hat, ld_band, genotypes)
    weights, scores = pl.pallas_call(
        hand_over,
        out_shape=(
            jax.ShapeDtypeStruct((TR, COLS), F32),
            jax.ShapeDtypeStruct((SHARE, 64), F32),
        ),
        in_specs=[vmem] * 2,
        out_specs=(vmem, vmem),
        name="hand_over",
        compiler_params=pltpu.CompilerParams(vmem_limit_bytes=60 << 20),
    )(weights, scores)
    return weights, scores.T


def solution(mesh):
    placed = (P("ind", "snp"), P("snp", None), P("snp"), P("ind"), P("ind", "snp"))
    return jax.shard_map(
        local,
        mesh=mesh,
        in_specs=placed,
        out_specs=(P("ind", "snp"), P(None, ("ind", "snp"))),
        check_vma=False,
    )
```

```python
import functools

import jax
import jax.numpy as jnp
from jax import lax
from jax.experimental import pallas as pl
from jax.experimental.pallas import tpu as pltpu
from jax.sharding import PartitionSpec as P

BLK = 128
M_GENOME = 1100000
N_GWAS = 1000000
SNP, IND = 32, 8
Y, Z, X = 4, 8, 4
NB = 8
TR = 8
COLS = NB * BLK
HALO = 512
SHARE = 32
MESH = pl.DeviceIdType.MESH
NT = (((1,), (1,)), ((), ()))
F32, BF16 = jnp.float32, jnp.bfloat16


def ring(n):
    return sorted(range(n), key=lambda k: -min(k, n - k))


SNP_OFFSETS = sorted(
    ((a, b) for a in range(Y) for b in range(Z) if (a, b) != (0, 0)),
    key=lambda q: -(min(q[0], Y - q[0]) + min(q[1], Z - q[1])),
)
CHIP_OFFSETS = sorted(
    ((a, b, c) for a in range(X) for b in range(Y) for c in range(Z) if (a, b, c) != (0, 0, 0)),
    key=lambda q: -(min(q[0], X - q[0]) + min(q[1], Y - q[1]) + min(q[2], Z - q[2])),
)
IND_OFFSETS = [(a, c) for a in ring(X) for c in (1, 0) if (a, c) != (0, 0)]


def split(value):
    high = value.astype(BF16).astype(F32)
    return jnp.concatenate([high, value - high], axis=0).astype(BF16)


def fold(out):
    return out[0:8, 0:BLK] + out[8:16, 0:BLK] + out[0:8, BLK:] + out[8:16, BLK:]


def window(padded, first, width, shift):
    segment = padded[:, first : first + width + BLK]
    return split(pltpu.roll(segment, width + BLK - shift, 1)[:, :width])


def product(b, vec, k0, hilo):
    out = lax.dot_general(
        vec, hilo[b, :, k0 : k0 + vec.shape[1]], NT, preferred_element_type=F32
    )
    return fold(out)


def local_part(value, shifts, hilo, acc):
    empty = jnp.zeros((TR, HALO), F32)
    padded = jnp.concatenate([empty, value, empty], axis=1)
    for b in range(NB):
        k0, k1 = max(0, 384 - BLK * b), min(COLS, 1536 - BLK * b)
        vec = window(padded, BLK * b + k0, k1 - k0, shifts[b])
        acc[:, b * BLK : (b + 1) * BLK] = product(b, vec, k0, hilo)


def halo_part(left, right, shifts, hilo, acc):
    empty = jnp.zeros((TR, BLK), F32)
    left = jnp.concatenate([left, empty], axis=1)
    right = jnp.concatenate([empty, right], axis=1)
    for b in range(NB):
        if b < 4:
            k0 = 0
            vec = window(left, BLK * b, HALO - BLK * b, shifts[b])
        else:
            k0 = 1408 - BLK * b
            vec = window(right, 0, COLS - k0, shifts[b])
        acc[:, b * BLK : (b + 1) * BLK] += product(b, vec, k0, hilo)


def wait_for(ref, sem):
    pltpu.make_async_copy(ref, ref, sem).wait()


def lane_sum(value):
    return jnp.sum(value, axis=1, keepdims=True)


def kernel(
    start_hbm,
    herit_hbm,
    beta_hbm,
    ld_ref,
    geno_ref,
    weights_out,
    scores_out,
    start_ref,
    herit_ref,
    beta_ref,
    ldbuf,
    hilo,
    geno,
    acc,
    ubuf,
    halo,
    basis,
    mom_own,
    mom_in,
    coef_own,
    coef_in,
    part,
    part_in,
    lines_in,
    line_own,
    line_in,
    stat_own,
    stat_in,
    weights_ref,
    scores_ref,
    ld_sem,
    geno_sem,
    small_sem,
    out_sem,
    halo_send,
    halo_recv,
    send_sem,
    recv_sem,
    word,
):
    s, i = lax.axis_index("snp"), lax.axis_index("ind")
    y, z, x, core = s // Z, s % Z, i // 2, i % 2

    def snp_peer(dy, dz):
        return lax.rem(y + dy, Y) * Z + lax.rem(z + dz, Z)

    def ind_peer(dx, dc):
        return lax.rem(x + dx, X) * 2 + lax.rem(core + dc, 2)

    near_peers = [(s, i + 1 - 2 * core)]
    far_peers = [
        (lax.rem(y + dy, Y) * Z + lax.rem(z + dz, Z), lax.rem(x + dx, X) * 2 + core)
        for dx, dy, dz in CHIP_OFFSETS
    ]

    def load(b):
        return pltpu.make_async_copy(ld_ref.at[pl.ds(b * BLK, BLK)], ldbuf.at[b], ld_sem.at[b])

    small = [
        pltpu.make_async_copy(src, dst, small_sem.at[k])
        for k, (src, dst) in enumerate(
            ((beta_hbm, beta_ref), (start_hbm, start_ref), (herit_hbm, herit_ref))
        )
    ]
    for copy in small:
        copy.start()
    for b in range(NB):
        load(b).start()
    load_geno = pltpu.make_async_copy(geno_ref, geno, geno_sem)
    load_geno.start()

    barrier = pltpu.get_barrier_semaphore()
    right, left = lax.rem(s + 1, SNP), lax.rem(s + SNP - 1, SNP)
    around_z = [(snp_peer(0, 1), i), (snp_peer(0, Z - 1), i)]
    around_y = [(snp_peer(dy, 0), i) for dy in range(1, Y)]
    beside = [(s, ind_peer(dx, dc)) for dx, dc in IND_OFFSETS]

    def signal(sem, peer):
        pl.semaphore_signal(sem, inc=1, device_id=peer, device_id_type=MESH)

    for peer in around_z + around_y + beside:
        signal(barrier, peer)

    @pl.when(z == Z - 1)
    def _():
        signal(barrier, (right, i))

    @pl.when(z == 0)
    def _():
        signal(barrier, (left, i))

    ends = jnp.where(lax.rem(z + 1, Z) < 2, 1, 0)
    pl.semaphore_wait(barrier, len(around_z + around_y + beside) + ends)

    steps = [
        around_z,
        [(snp_peer(0, 2), i), (snp_peer(0, Z - 2), i)],
        around_y,
    ]

    def tell(step):
        for peer in steps[step]:
            signal(word.at[step], peer)

    def hear(step):
        pl.semaphore_wait(word.at[step], len(steps[step]))

    tell(0)

    for copy in small:
        copy.wait()
    def send_halo(src, turn):
        copies = [
            pltpu.make_async_remote_copy(
                src_ref=src.at[:, COLS - HALO :],
                dst_ref=halo.at[turn, 0],
                send_sem=halo_send.at[turn, 0],
                recv_sem=halo_recv.at[turn, 0],
                device_id=(right, i),
                device_id_type=MESH,
            ),
            pltpu.make_async_remote_copy(
                src_ref=src.at[:, :HALO],
                dst_ref=halo.at[turn, 1],
                send_sem=halo_send.at[turn, 1],
                recv_sem=halo_recv.at[turn, 1],
                device_id=(left, i),
                device_id_type=MESH,
            ),
        ]
        for copy in copies:
            copy.start()
            pending.append(copy.wait_send)
        return copies

    pending = []
    halo0 = send_halo(beta_ref, 0)
    beta = beta_ref[...]

    def gather(turn, parts):
        basis[turn, i] = parts
        for dx, dc in IND_OFFSETS:
            pltpu.make_async_remote_copy(
                src_ref=basis.at[turn, i],
                dst_ref=basis.at[turn, i],
                send_sem=send_sem.at[turn],
                recv_sem=recv_sem.at[turn],
                device_id=(s, ind_peer(dx, dc)),
                device_id_type=MESH,
            ).start()
        pending.append(lambda: wait_for(basis.at[turn, 0 : len(IND_OFFSETS)], send_sem.at[turn]))

    beta_parts = split(beta)
    gather(0, beta_parts)

    shifts = [start_ref[b] - (BLK * (s * NB + b) - HALO) for b in range(NB)]
    for b in range(NB):
        load(b).wait()

        def rows(k, carry, b=b):
            r0 = pl.multiple_of(k * 32, 32)
            value = ldbuf[b, pl.ds(r0, 32), :]
            high = value.astype(BF16)
            hilo[b, pl.ds(r0, 32), :] = high
            hilo[b, pl.ds(BLK + r0, 32), :] = (value - high.astype(F32)).astype(BF16)
            return carry

        lax.fori_loop(0, BLK // 32, rows, 0)

    def off_diagonal(parts, turn, copies):
        for copy in copies:
            copy.wait_recv()
        halo_part(halo[turn, 0], halo[turn, 1], shifts, hilo, acc)
        return acc[...] - (parts[0:8].astype(F32) + parts[8:16].astype(F32))

    local_part(beta, shifts, hilo, acc)
    hear(0)
    tell(1)
    u = off_diagonal(beta_parts, 0, halo0)
    u_parts = split(u)
    gather(1, u_parts)
    ubuf[...] = u
    halo1 = send_halo(ubuf, 1)
    hear(1)
    tell(2)

    slot = {offset: j for j, offset in enumerate(SNP_OFFSETS)}
    lane = lax.broadcasted_iota(jnp.int32, (1, BLK), 1)
    half = lane < 64

    def both(value):
        return value + pltpu.roll(value, 64, value.ndim - 1)

    def partial_scores(turn):
        wait_for(basis.at[turn, 0 : len(IND_OFFSETS)], recv_sem.at[turn])
        every = basis[turn].astype(F32)
        every = jnp.concatenate(
            [every[:, 0:8].reshape(64, COLS), every[:, 8:16].reshape(64, COLS)], axis=0
        ).astype(BF16)
        for dy in ring(Y):
            group = lax.rem(y + dy, Y)
            rows = geno[pl.ds(pl.multiple_of(group * 256, 256), 256), :]
            out = both(lax.dot_general(rows, every, NT, preferred_element_type=F32))
            out = out.reshape(Z, 2, 16, BLK)
            part[turn, pl.ds(group * Z, Z)] = jnp.where(half, out[:, 0], out[:, 1])
            if turn == 0:
                if dy:
                    along_y(dy)
                continue
            for dz in ring(Z):
                if (dy, dz) != (0, 0):
                    peer = group * Z + lax.rem(z + dz, Z)
                    pltpu.make_async_remote_copy(
                        src_ref=part.at[turn, peer],
                        dst_ref=part_in.at[slot[dy, dz]],
                        send_sem=send_sem.at[3],
                        recv_sem=recv_sem.at[3],
                        device_id=(peer, i),
                        device_id_type=MESH,
                    ).start()
        if turn == 1:
            pending.append(lambda: wait_for(part_in, send_sem.at[3]))

    def along_y(dy):
        group = lax.rem(y + dy, Y)
        pltpu.make_async_remote_copy(
            src_ref=part.at[0, pl.ds(group * Z, Z)],
            dst_ref=lines_in.at[dy - 1],
            send_sem=send_sem.at[2],
            recv_sem=recv_sem.at[2],
            device_id=(group * Z + z, i),
            device_id_type=MESH,
        ).start()

    def along_z():
        wait_for(lines_in, recv_sem.at[2])
        line_own[...] = part[0, pl.ds(y * Z, Z)] + jnp.sum(lines_in[...], axis=0)
        for dz in ring(Z)[:-1]:
            peer = lax.rem(z + dz, Z)
            pltpu.make_async_remote_copy(
                src_ref=line_own.at[peer],
                dst_ref=line_in.at[dz - 1],
                send_sem=send_sem.at[8],
                recv_sem=recv_sem.at[8],
                device_id=(y * Z + peer, i),
                device_id_type=MESH,
            ).start()
        pending.append(lambda: wait_for(lines_in, send_sem.at[2]))
        pending.append(lambda: wait_for(line_in, send_sem.at[8]))

    def total_scores(turn):
        if turn == 0:
            wait_for(line_in, recv_sem.at[8])
            return line_own[z] + jnp.sum(line_in[...], axis=0)
        wait_for(part_in, recv_sem.at[3])
        return part[1, s] + jnp.sum(part_in[...], axis=0)

    load_geno.wait()
    partial_scores(0)

    local_part(u, shifts, hilo, acc)
    p0 = lane_sum(beta * beta)
    p1 = lane_sum(beta * u)
    theta = jnp.where(p0 > 0, p1 / p0, 0.0)
    e = u - theta * beta
    q = lane_sum(e * e)
    t = lane_sum(e * beta)

    g = off_diagonal(u_parts, 1, halo1) - theta * u
    f = lane_sum(e * g)
    h = lane_sum(beta * g)
    tile_lane = lax.broadcasted_iota(jnp.int32, (TR, BLK), 1)
    tile_row = lax.broadcasted_iota(jnp.int32, (TR, BLK), 0)
    tile = jnp.broadcast_to(p0, (TR, BLK))
    for k, value in enumerate((theta, q, t, f, h)):
        tile = jnp.where(tile_lane >= 16 * (k + 1), value, tile)
    tile = jnp.where(tile_lane % 16 == tile_row, tile, 0.0)
    sums = jnp.sum(tile, axis=0, keepdims=True)
    hear(2)
    mom_own[...] = sums
    mom_in[len(SNP_OFFSETS)] = sums
    for j, (dy, dz) in enumerate(SNP_OFFSETS):
        pltpu.make_async_remote_copy(
            src_ref=mom_own,
            dst_ref=mom_in.at[j],
            send_sem=send_sem.at[4],
            recv_sem=recv_sem.at[4],
            device_id=(snp_peer(dy, dz), i),
            device_id_type=MESH,
        ).start()

    pending.append(lambda: wait_for(mom_in.at[0 : len(SNP_OFFSETS)], send_sem.at[4]))

    partial_scores(1)
    along_z()

    herit = jnp.ones((1, BLK), F32)
    for k in range(TR):
        herit = jnp.where(lane == k, herit_ref[k], herit)
    kappa = 1.0 + (M_GENOME / N_GWAS) / herit

    wait_for(mom_in.at[0 : len(SNP_OFFSETS)], recv_sem.at[4])
    moments = mom_in[...]
    p0_d, th_d, q_d, t_d, f_d, h_d = [
        moments if k == 0 else pltpu.roll(moments, BLK - 16 * k, 2) for k in range(6)
    ]
    p0 = jnp.sum(p0_d, axis=0)
    theta = jnp.sum(p0_d * th_d + t_d, axis=0) / p0
    delta = th_d - theta[None]
    q = jnp.sum(q_d + delta * (2.0 * t_d + delta * p0_d), axis=0)
    t = jnp.sum(t_d + delta * p0_d, axis=0)
    f = jnp.sum(
        f_d + delta * (q_d + th_d * t_d + h_d + delta * (t_d + th_d * p0_d)), axis=0
    )
    a11 = p0 * (theta + kappa)
    a12 = q + (theta + kappa) * t
    a22 = f + kappa * q
    det = a11 * a22 - a12 * a12
    c1 = jnp.where(det > 0, (t * a11 - p0 * a12) / det, 0.0)
    c0 = (p0 - c1 * a12) / a11 - c1 * theta

    own_lanes = lane < TR
    coef = jnp.where(own_lanes, c0, 0.0) + pltpu.roll(jnp.where(own_lanes, c1, 0.0), 64, 1)
    coef = pltpu.roll(coef, i * TR, 1)
    coef_own[...] = coef
    coef_in[len(IND_OFFSETS)] = coef
    for j, (dx, dc) in enumerate(IND_OFFSETS):
        pltpu.make_async_remote_copy(
            src_ref=coef_own,
            dst_ref=coef_in.at[j],
            send_sem=send_sem.at[5],
            recv_sem=recv_sem.at[5],
            device_id=(s, ind_peer(dx, dc)),
            device_id_type=MESH,
        ).start()

    pending.append(lambda: wait_for(coef_in.at[0 : len(IND_OFFSETS)], send_sem.at[5]))

    diagonal = tile_lane == tile_row
    c0 = lane_sum(jnp.where(diagonal, c0, 0.0))
    c1 = lane_sum(jnp.where(diagonal, c1, 0.0))
    weights_ref[...] = c0 * beta + c1 * u
    store_weights = pltpu.make_async_copy(weights_ref, weights_out, out_sem.at[0])
    store_weights.start()

    beta_scores = total_scores(0)
    wait_for(coef_in.at[0 : len(IND_OFFSETS)], recv_sem.at[5])
    coef = jnp.sum(coef_in[...], axis=0)
    swapped = pltpu.roll(coef, 64, 1)
    beta_scores = beta_scores * jnp.where(half, coef, swapped)
    raw = beta_scores + total_scores(1) * jnp.where(half, swapped, coef)

    mean = both(jnp.sum(raw, axis=0, keepdims=True)) * (1.0 / SHARE)
    spread = both(jnp.sum((raw - mean) * (raw - mean), axis=0, keepdims=True))
    stat = jnp.where(half, mean, spread)
    size = SHARE
    for turn, peers in enumerate((near_peers, far_peers)):
        count = len(peers) + 1
        stat_own[turn] = stat
        stat_in[turn, len(peers)] = stat
        for j, peer in enumerate(peers):
            pltpu.make_async_remote_copy(
                src_ref=stat_own.at[turn],
                dst_ref=stat_in.at[turn, j],
                send_sem=send_sem.at[6 + turn],
                recv_sem=recv_sem.at[6 + turn],
                device_id=peer,
                device_id_type=MESH,
            ).start()
        arrived = stat_in.at[turn, 0 : len(peers)]
        pending.append(lambda turn=turn, arrived=arrived: wait_for(arrived, send_sem.at[6 + turn]))
        wait_for(arrived, recv_sem.at[6 + turn])
        values = stat_in[turn, 0:count]
        total = jnp.sum(values, axis=0)
        mean = total * (1.0 / count)
        apart = jnp.where(half, values - mean, 0.0)
        squares = jnp.sum(apart * apart, axis=0) * float(size)
        stat = jnp.where(half, mean, total + pltpu.roll(squares, 64, 1))
        size *= count
    swapped = pltpu.roll(stat, 64, 1)
    mean = jnp.where(half, stat, swapped)
    variance = jnp.where(half, swapped, stat) * (1.0 / size)
    scores = (raw - mean) * lax.rsqrt(variance + 1e-05)
    scores_ref[0:16, :] = scores[:, 0:64]
    scores_ref[16:32, :] = scores[:, 64:128]
    store_scores = pltpu.make_async_copy(scores_ref, scores_out, out_sem.at[1])
    store_scores.start()

    for drain in pending:
        drain()
    store_weights.wait()
    store_scores.wait()


def hand_over(weights_ref, scores_ref, weights_out, scores_out):
    weights_out[...] = weights_ref[...]
    scores_out[...] = scores_ref[...]


def local(beta_hat, ld_band, band_start, heritability, genotypes):
    vmem, anywhere = pl.BlockSpec(memory_space=pltpu.VMEM), pl.BlockSpec(memory_space=pl.ANY)
    dma = pltpu.SemaphoreType.DMA
    weights, scores = pl.pallas_call(
        kernel,
        out_shape=(
            jax.ShapeDtypeStruct((TR, COLS), F32),
            jax.ShapeDtypeStruct((SHARE, 64), F32),
        ),
        in_specs=[anywhere] * 5,
        out_specs=(anywhere, anywhere),
        scratch_shapes=[
            pltpu.SMEM((NB,), jnp.int32),
            pltpu.SMEM((TR,), F32),
            pltpu.VMEM((TR, COLS), F32),
            pltpu.VMEM((NB, BLK, COLS), F32),
            pltpu.VMEM((NB, 2 * BLK, COLS), BF16),
            pltpu.VMEM((1024, COLS), BF16),
            pltpu.VMEM((TR, COLS), F32),
            pltpu.VMEM((TR, COLS), F32),
            pltpu.VMEM((2, 2, TR, HALO), F32),
            pltpu.VMEM((2, IND, 16, COLS), BF16),
            pltpu.VMEM((1, BLK), F32),
            pltpu.VMEM((SNP, 1, BLK), F32),
            pltpu.VMEM((1, BLK), F32),
            pltpu.VMEM((IND, 1, BLK), F32),
            pltpu.VMEM((2, SNP, 16, BLK), F32),
            pltpu.VMEM((SNP - 1, 16, BLK), F32),
            pltpu.VMEM((Y - 1, Z, 16, BLK), F32),
            pltpu.VMEM((Z, 16, BLK), F32),
            pltpu.VMEM((Z - 1, 16, BLK), F32),
            pltpu.VMEM((2, 1, BLK), F32),
            pltpu.VMEM((2, X * Y * Z, 1, BLK), F32),
            pltpu.VMEM((TR, COLS), F32),
            pltpu.VMEM((SHARE, 64), F32),
            dma((NB,)),
            dma,
            dma((3,)),
            dma((2,)),
            dma((2, 2)),
            dma((2, 2)),
            dma((9,)),
            dma((9,)),
            pltpu.SemaphoreType.REGULAR((3,)),
        ],
        name="ldpred_scores",
        compiler_params=pltpu.CompilerParams(
            collective_id=0, has_side_effects=True, vmem_limit_bytes=60 << 20
        ),
    )(band_start, heritability, beta_hat, ld_band, genotypes)
    weights, scores = pl.pallas_call(
        hand_over,
        out_shape=(
            jax.ShapeDtypeStruct((TR, COLS), F32),
            jax.ShapeDtypeStruct((SHARE, 64), F32),
        ),
        in_specs=[vmem] * 2,
        out_specs=(vmem, vmem),
        name="hand_over",
        compiler_params=pltpu.CompilerParams(vmem_limit_bytes=60 << 20),
    )(weights, scores)
    return weights, scores.T


def solution(mesh):
    placed = (P("ind", "snp"), P("snp", None), P("snp"), P("ind"), P("ind", "snp"))
    return jax.shard_map(
        local,
        mesh=mesh,
        in_specs=placed,
        out_specs=(P("ind", "snp"), P(None, ("ind", "snp"))),
        check_vma=False,
    )
```

```python
import functools

import jax
import jax.numpy as jnp
from jax import lax
from jax.experimental import pallas as pl
from jax.experimental.pallas import tpu as pltpu
from jax.sharding import PartitionSpec as P

BLK = 128
M_GENOME = 1100000
N_GWAS = 1000000
SNP, IND = 32, 8
Y, Z, X = 4, 8, 4
NB = 8
TR = 8
COLS = NB * BLK
HALO = 512
SHARE = 32
MESH = pl.DeviceIdType.MESH
NT = (((1,), (1,)), ((), ()))
F32, BF16 = jnp.float32, jnp.bfloat16


def ring(n):
    return sorted(range(n), key=lambda k: -min(k, n - k))


SNP_OFFSETS = sorted(
    ((a, b) for a in range(Y) for b in range(Z) if (a, b) != (0, 0)),
    key=lambda q: -(min(q[0], Y - q[0]) + min(q[1], Z - q[1])),
)
ALL_OFFSETS = sorted(
    ((a, b, c, d) for a in range(X) for b in range(Y) for c in range(Z) for d in range(2)),
    key=lambda q: -(min(q[0], X - q[0]) + min(q[1], Y - q[1]) + min(q[2], Z - q[2])) - q[3] / 2,
)[:-1]
IND_OFFSETS = [(a, c) for a in ring(X) for c in (1, 0) if (a, c) != (0, 0)]


def split(value):
    high = value.astype(BF16).astype(F32)
    return jnp.concatenate([high, value - high], axis=0).astype(BF16)


def fold(out):
    return out[0:8, 0:BLK] + out[8:16, 0:BLK] + out[0:8, BLK:] + out[8:16, BLK:]


def window(padded, first, width, shift):
    segment = padded[:, first : first + width + BLK]
    return split(pltpu.roll(segment, width + BLK - shift, 1)[:, :width])


def product(b, vec, k0, hilo):
    out = lax.dot_general(
        vec, hilo[b, :, k0 : k0 + vec.shape[1]], NT, preferred_element_type=F32
    )
    return fold(out)


def local_part(value, shifts, hilo, acc):
    empty = jnp.zeros((TR, HALO), F32)
    padded = jnp.concatenate([empty, value, empty], axis=1)
    for b in range(NB):
        k0, k1 = max(0, 384 - BLK * b), min(COLS, 1536 - BLK * b)
        vec = window(padded, BLK * b + k0, k1 - k0, shifts[b])
        acc[:, b * BLK : (b + 1) * BLK] = product(b, vec, k0, hilo)


def halo_part(left, right, shifts, hilo, acc):
    empty = jnp.zeros((TR, BLK), F32)
    left = jnp.concatenate([left, empty], axis=1)
    right = jnp.concatenate([empty, right], axis=1)
    for b in range(NB):
        if b < 4:
            k0 = 0
            vec = window(left, BLK * b, HALO - BLK * b, shifts[b])
        else:
            k0 = 1408 - BLK * b
            vec = window(right, 0, COLS - k0, shifts[b])
        acc[:, b * BLK : (b + 1) * BLK] += product(b, vec, k0, hilo)


def wait_for(ref, sem):
    pltpu.make_async_copy(ref, ref, sem).wait()


def row_sum(value):
    return jnp.sum(value, axis=0, keepdims=True)


def lane_sum(value):
    return jnp.sum(value, axis=1, keepdims=True)


def kernel(
    start_hbm,
    herit_hbm,
    beta_hbm,
    ld_ref,
    geno_ref,
    weights_out,
    scores_out,
    start_ref,
    herit_ref,
    beta_ref,
    ldbuf,
    hilo,
    geno,
    acc,
    ubuf,
    halo,
    basis,
    mom_own,
    mom_in,
    coef_own,
    coef_in,
    part,
    part_in,
    lines_in,
    line_own,
    line_in,
    stat_own,
    stat_in,
    weights_ref,
    scores_ref,
    ld_sem,
    geno_sem,
    small_sem,
    out_sem,
    halo_send,
    halo_recv,
    send_sem,
    recv_sem,
    word,
):
    s, i = lax.axis_index("snp"), lax.axis_index("ind")
    y, z, x, core = s // Z, s % Z, i // 2, i % 2

    def snp_peer(dy, dz):
        return lax.rem(y + dy, Y) * Z + lax.rem(z + dz, Z)

    def ind_peer(dx, dc):
        return lax.rem(x + dx, X) * 2 + lax.rem(core + dc, 2)

    everyone = [
        (snp_peer(dy, dz), ind_peer(dx, dc)) for dx, dy, dz, dc in ALL_OFFSETS
    ]

    def load(b):
        return pltpu.make_async_copy(ld_ref.at[pl.ds(b * BLK, BLK)], ldbuf.at[b], ld_sem.at[b])

    barrier = pltpu.get_barrier_semaphore()
    right, left = lax.rem(s + 1, SNP), lax.rem(s + SNP - 1, SNP)
    around_z = [(snp_peer(0, 1), i), (snp_peer(0, Z - 1), i)]
    around_y = [(snp_peer(dy, 0), i) for dy in range(1, Y)]
    beside = [(s, ind_peer(dx, dc)) for dx, dc in IND_OFFSETS]

    def signal(sem, peer):
        pl.semaphore_signal(sem, inc=1, device_id=peer, device_id_type=MESH)

    for peer in around_z + around_y + beside:
        signal(barrier, peer)

    @pl.when(z == Z - 1)
    def _():
        signal(barrier, (right, i))

    @pl.when(z == 0)
    def _():
        signal(barrier, (left, i))

    small = [
        pltpu.make_async_copy(src, dst, small_sem.at[k])
        for k, (src, dst) in enumerate(
            ((beta_hbm, beta_ref), (start_hbm, start_ref), (herit_hbm, herit_ref))
        )
    ]
    for copy in small:
        copy.start()
    for b in range(NB):
        load(b).start()
    load_geno = pltpu.make_async_copy(geno_ref, geno, geno_sem)
    load_geno.start()

    ends = jnp.where(lax.rem(z + 1, Z) < 2, 1, 0)
    pl.semaphore_wait(barrier, len(around_z + around_y + beside) + ends)

    steps = [
        around_z,
        [(snp_peer(0, 2), i), (snp_peer(0, Z - 2), i)],
        around_y,
    ]

    def tell(step):
        for peer in steps[step]:
            signal(word.at[step], peer)

    def hear(step):
        pl.semaphore_wait(word.at[step], len(steps[step]))

    tell(0)

    for copy in small:
        copy.wait()
    def send_halo(src, turn):
        copies = [
            pltpu.make_async_remote_copy(
                src_ref=src.at[:, COLS - HALO :],
                dst_ref=halo.at[turn, 0],
                send_sem=halo_send.at[turn, 0],
                recv_sem=halo_recv.at[turn, 0],
                device_id=(right, i),
                device_id_type=MESH,
            ),
            pltpu.make_async_remote_copy(
                src_ref=src.at[:, :HALO],
                dst_ref=halo.at[turn, 1],
                send_sem=halo_send.at[turn, 1],
                recv_sem=halo_recv.at[turn, 1],
                device_id=(left, i),
                device_id_type=MESH,
            ),
        ]
        for copy in copies:
            copy.start()
            pending.append(copy.wait_send)
        return copies

    pending = []
    halo0 = send_halo(beta_ref, 0)
    beta = beta_ref[...]

    def gather(turn, parts):
        basis[turn, i] = parts
        for dx, dc in IND_OFFSETS:
            pltpu.make_async_remote_copy(
                src_ref=basis.at[turn, i],
                dst_ref=basis.at[turn, i],
                send_sem=send_sem.at[turn],
                recv_sem=recv_sem.at[turn],
                device_id=(s, ind_peer(dx, dc)),
                device_id_type=MESH,
            ).start()
        pending.append(lambda: wait_for(basis.at[turn, 0 : len(IND_OFFSETS)], send_sem.at[turn]))

    beta_parts = split(beta)
    gather(0, beta_parts)

    shifts = [start_ref[b] - (BLK * (s * NB + b) - HALO) for b in range(NB)]
    for b in range(NB):
        load(b).wait()

        def rows(k, carry, b=b):
            r0 = pl.multiple_of(k * 32, 32)
            value = ldbuf[b, pl.ds(r0, 32), :]
            high = value.astype(BF16)
            hilo[b, pl.ds(r0, 32), :] = high
            hilo[b, pl.ds(BLK + r0, 32), :] = (value - high.astype(F32)).astype(BF16)
            return carry

        lax.fori_loop(0, BLK // 32, rows, 0)

    def off_diagonal(parts, turn, copies):
        for copy in copies:
            copy.wait_recv()
        halo_part(halo[turn, 0], halo[turn, 1], shifts, hilo, acc)
        return acc[...] - (parts[0:8].astype(F32) + parts[8:16].astype(F32))

    local_part(beta, shifts, hilo, acc)
    hear(0)
    tell(1)
    u = off_diagonal(beta_parts, 0, halo0)
    u_parts = split(u)
    gather(1, u_parts)
    ubuf[...] = u
    halo1 = send_halo(ubuf, 1)
    hear(1)
    tell(2)

    slot = {offset: j for j, offset in enumerate(SNP_OFFSETS)}
    lane = lax.broadcasted_iota(jnp.int32, (1, BLK), 1)
    half = lane < 64

    def both(value):
        return value + pltpu.roll(value, 64, value.ndim - 1)

    def partial_scores(turn):
        wait_for(basis.at[turn, 0 : len(IND_OFFSETS)], recv_sem.at[turn])
        every = basis[turn].astype(F32)
        every = jnp.concatenate(
            [every[:, 0:8].reshape(64, COLS), every[:, 8:16].reshape(64, COLS)], axis=0
        ).astype(BF16)
        for dy in ring(Y):
            group = lax.rem(y + dy, Y)
            rows = geno[pl.ds(pl.multiple_of(group * 256, 256), 256), :]
            out = both(lax.dot_general(rows, every, NT, preferred_element_type=F32))
            out = out.reshape(Z, 2, 16, BLK)
            part[turn, pl.ds(group * Z, Z)] = jnp.where(half, out[:, 0], out[:, 1])
            if turn == 0:
                if dy:
                    along_y(dy)
                continue
            for dz in ring(Z):
                if (dy, dz) != (0, 0):
                    peer = group * Z + lax.rem(z + dz, Z)
                    pltpu.make_async_remote_copy(
                        src_ref=part.at[turn, peer],
                        dst_ref=part_in.at[slot[dy, dz]],
                        send_sem=send_sem.at[3],
                        recv_sem=recv_sem.at[3],
                        device_id=(peer, i),
                        device_id_type=MESH,
                    ).start()
        if turn == 1:
            pending.append(lambda: wait_for(part_in, send_sem.at[3]))

    def along_y(dy):
        group = lax.rem(y + dy, Y)
        pltpu.make_async_remote_copy(
            src_ref=part.at[0, pl.ds(group * Z, Z)],
            dst_ref=lines_in.at[dy - 1],
            send_sem=send_sem.at[2],
            recv_sem=recv_sem.at[2],
            device_id=(group * Z + z, i),
            device_id_type=MESH,
        ).start()

    def along_z():
        wait_for(lines_in, recv_sem.at[2])
        line_own[...] = part[0, pl.ds(y * Z, Z)] + jnp.sum(lines_in[...], axis=0)
        for dz in ring(Z)[:-1]:
            peer = lax.rem(z + dz, Z)
            pltpu.make_async_remote_copy(
                src_ref=line_own.at[peer],
                dst_ref=line_in.at[dz - 1],
                send_sem=send_sem.at[8],
                recv_sem=recv_sem.at[8],
                device_id=(y * Z + peer, i),
                device_id_type=MESH,
            ).start()
        pending.append(lambda: wait_for(lines_in, send_sem.at[2]))
        pending.append(lambda: wait_for(line_in, send_sem.at[8]))

    def total_scores(turn):
        if turn == 0:
            wait_for(line_in, recv_sem.at[8])
            return line_own[z] + jnp.sum(line_in[...], axis=0)
        wait_for(part_in, recv_sem.at[3])
        return part[1, s] + jnp.sum(part_in[...], axis=0)

    load_geno.wait()
    partial_scores(0)

    local_part(u, shifts, hilo, acc)
    p0 = lane_sum(beta * beta)
    p1 = lane_sum(beta * u)
    theta = jnp.where(p0 > 0, p1 / p0, 0.0)
    e = u - theta * beta
    q = lane_sum(e * e)
    t = lane_sum(e * beta)

    g = off_diagonal(u_parts, 1, halo1) - theta * u
    f = lane_sum(e * g)
    h = lane_sum(beta * g)
    tile_lane = lax.broadcasted_iota(jnp.int32, (TR, BLK), 1)
    tile_row = lax.broadcasted_iota(jnp.int32, (TR, BLK), 0)
    tile = jnp.broadcast_to(p0, (TR, BLK))
    for k, value in enumerate((theta, q, t, f, h)):
        tile = jnp.where(tile_lane >= 16 * (k + 1), value, tile)
    tile = jnp.where(tile_lane % 16 == tile_row, tile, 0.0)
    sums = jnp.sum(tile, axis=0, keepdims=True)
    hear(2)
    mom_own[...] = sums
    mom_in[SNP - 1 :] = sums
    for j, (dy, dz) in enumerate(SNP_OFFSETS):
        pltpu.make_async_remote_copy(
            src_ref=mom_own,
            dst_ref=mom_in.at[pl.ds(j, 1)],
            send_sem=send_sem.at[4],
            recv_sem=recv_sem.at[4],
            device_id=(snp_peer(dy, dz), i),
            device_id_type=MESH,
        ).start()

    pending.append(lambda: wait_for(mom_in.at[0 : len(SNP_OFFSETS)], send_sem.at[4]))

    partial_scores(1)
    along_z()

    herit = jnp.ones((1, BLK), F32)
    for k in range(TR):
        herit = jnp.where(lane == k, herit_ref[k], herit)
    kappa = 1.0 + (M_GENOME / N_GWAS) / herit

    wait_for(mom_in.at[0 : len(SNP_OFFSETS)], recv_sem.at[4])
    moments = mom_in[...]
    p0_d, th_d, q_d, t_d, f_d, h_d = [
        moments if k == 0 else pltpu.roll(moments, BLK - 16 * k, 1) for k in range(6)
    ]
    p0 = row_sum(p0_d)
    theta = row_sum(p0_d * th_d + t_d) / p0
    delta = th_d - theta
    q = row_sum(q_d + delta * (2.0 * t_d + delta * p0_d))
    t = row_sum(t_d + delta * p0_d)
    f = row_sum(f_d + delta * (q_d + th_d * t_d + h_d + delta * (t_d + th_d * p0_d)))
    a11 = p0 * (theta + kappa)
    a12 = q + (theta + kappa) * t
    a22 = f + kappa * q
    det = a11 * a22 - a12 * a12
    c1 = jnp.where(det > 0, (t * a11 - p0 * a12) / det, 0.0)
    c0 = (p0 - c1 * a12) / a11 - c1 * theta

    own_lanes = lane < TR
    coef = jnp.where(own_lanes, c0, 0.0) + pltpu.roll(jnp.where(own_lanes, c1, 0.0), 64, 1)
    coef = pltpu.roll(coef, i * TR, 1)
    coef_own[...] = coef
    coef_in[IND - 1 :] = coef
    for j, (dx, dc) in enumerate(IND_OFFSETS):
        pltpu.make_async_remote_copy(
            src_ref=coef_own,
            dst_ref=coef_in.at[pl.ds(j, 1)],
            send_sem=send_sem.at[5],
            recv_sem=recv_sem.at[5],
            device_id=(s, ind_peer(dx, dc)),
            device_id_type=MESH,
        ).start()

    pending.append(lambda: wait_for(coef_in.at[0 : len(IND_OFFSETS)], send_sem.at[5]))

    diagonal = tile_lane == tile_row
    c0 = lane_sum(jnp.where(diagonal, c0, 0.0))
    c1 = lane_sum(jnp.where(diagonal, c1, 0.0))
    weights_ref[...] = c0 * beta + c1 * u
    store_weights = pltpu.make_async_copy(weights_ref, weights_out, out_sem.at[0])
    store_weights.start()

    beta_scores = total_scores(0)
    wait_for(coef_in.at[0 : len(IND_OFFSETS)], recv_sem.at[5])
    coef = row_sum(coef_in[...])
    swapped = pltpu.roll(coef, 64, 1)
    beta_scores = beta_scores * jnp.where(half, coef, swapped)
    raw = beta_scores + total_scores(1) * jnp.where(half, swapped, coef)

    mean = both(jnp.sum(raw, axis=0, keepdims=True)) * (1.0 / SHARE)
    spread = both(jnp.sum((raw - mean) * (raw - mean), axis=0, keepdims=True))
    stat = jnp.where(half, mean, spread)
    count = len(everyone) + 1
    stat_own[...] = stat
    stat_in[len(everyone) :] = stat
    for j, peer in enumerate(everyone):
        pltpu.make_async_remote_copy(
            src_ref=stat_own,
            dst_ref=stat_in.at[pl.ds(j, 1)],
            send_sem=send_sem.at[6],
            recv_sem=recv_sem.at[6],
            device_id=peer,
            device_id_type=MESH,
        ).start()
    arrived = stat_in.at[0 : len(everyone)]
    pending.append(lambda: wait_for(arrived, send_sem.at[6]))
    wait_for(arrived, recv_sem.at[6])
    values = stat_in[...]
    total = row_sum(values)
    mean = total * (1.0 / count)
    apart = jnp.where(half, values - mean, 0.0)
    squares = row_sum(apart * apart) * float(SHARE)
    stat = jnp.where(half, mean, total + pltpu.roll(squares, 64, 1))
    size = SHARE * count
    swapped = pltpu.roll(stat, 64, 1)
    mean = jnp.where(half, stat, swapped)
    variance = jnp.where(half, swapped, stat) * (1.0 / size)
    scores = (raw - mean) * lax.rsqrt(variance + 1e-05)
    scores_ref[0:16, :] = scores[:, 0:64]
    scores_ref[16:32, :] = scores[:, 64:128]
    store_scores = pltpu.make_async_copy(scores_ref, scores_out, out_sem.at[1])
    store_scores.start()

    for drain in pending:
        drain()
    store_weights.wait()
    store_scores.wait()


def hand_over(weights_ref, scores_ref, weights_out, scores_out):
    weights_out[...] = weights_ref[...]
    scores_out[...] = scores_ref[...]


def local(beta_hat, ld_band, band_start, heritability, genotypes):
    vmem, anywhere = pl.BlockSpec(memory_space=pltpu.VMEM), pl.BlockSpec(memory_space=pl.ANY)
    dma = pltpu.SemaphoreType.DMA
    weights, scores = pl.pallas_call(
        kernel,
        out_shape=(
            jax.ShapeDtypeStruct((TR, COLS), F32),
            jax.ShapeDtypeStruct((SHARE, 64), F32),
        ),
        in_specs=[anywhere] * 5,
        out_specs=(anywhere, anywhere),
        scratch_shapes=[
            pltpu.SMEM((NB,), jnp.int32),
            pltpu.SMEM((TR,), F32),
            pltpu.VMEM((TR, COLS), F32),
            pltpu.VMEM((NB, BLK, COLS), F32),
            pltpu.VMEM((NB, 2 * BLK, COLS), BF16),
            pltpu.VMEM((1024, COLS), BF16),
            pltpu.VMEM((TR, COLS), F32),
            pltpu.VMEM((TR, COLS), F32),
            pltpu.VMEM((2, 2, TR, HALO), F32),
            pltpu.VMEM((2, IND, 16, COLS), BF16),
            pltpu.VMEM((1, BLK), F32),
            pltpu.VMEM((SNP, BLK), F32),
            pltpu.VMEM((1, BLK), F32),
            pltpu.VMEM((IND, BLK), F32),
            pltpu.VMEM((2, SNP, 16, BLK), F32),
            pltpu.VMEM((SNP - 1, 16, BLK), F32),
            pltpu.VMEM((Y - 1, Z, 16, BLK), F32),
            pltpu.VMEM((Z, 16, BLK), F32),
            pltpu.VMEM((Z - 1, 16, BLK), F32),
            pltpu.VMEM((1, BLK), F32),
            pltpu.VMEM((SNP * IND, BLK), F32),
            pltpu.VMEM((TR, COLS), F32),
            pltpu.VMEM((SHARE, 64), F32),
            dma((NB,)),
            dma,
            dma((3,)),
            dma((2,)),
            dma((2, 2)),
            dma((2, 2)),
            dma((9,)),
            dma((9,)),
            pltpu.SemaphoreType.REGULAR((3,)),
        ],
        name="ldpred_scores",
        compiler_params=pltpu.CompilerParams(
            collective_id=0, has_side_effects=True, vmem_limit_bytes=60 << 20
        ),
    )(band_start, heritability, beta_hat, ld_band, genotypes)
    weights, scores = pl.pallas_call(
        hand_over,
        out_shape=(
            jax.ShapeDtypeStruct((TR, COLS), F32),
            jax.ShapeDtypeStruct((SHARE, 64), F32),
        ),
        in_specs=[vmem] * 2,
        out_specs=(vmem, vmem),
        name="hand_over",
        compiler_params=pltpu.CompilerParams(vmem_limit_bytes=60 << 20),
    )(weights, scores)
    return weights, scores.T


def solution(mesh):
    placed = (P("ind", "snp"), P("snp", None), P("snp"), P("ind"), P("ind", "snp"))
    return jax.shard_map(
        local,
        mesh=mesh,
        in_specs=placed,
        out_specs=(P("ind", "snp"), P(None, ("ind", "snp"))),
        check_vma=False,
    )
```

```python
import functools

import jax
import jax.numpy as jnp
from jax import lax
from jax.experimental import pallas as pl
from jax.experimental.pallas import tpu as pltpu
from jax.sharding import PartitionSpec as P

BLK = 128
M_GENOME = 1100000
N_GWAS = 1000000
SNP, IND = 32, 8
Y, Z, X = 4, 8, 4
NB = 8
TR = 8
COLS = NB * BLK
HALO = 512
SHARE = 32
MESH = pl.DeviceIdType.MESH
NT = (((1,), (1,)), ((), ()))
F32, BF16 = jnp.float32, jnp.bfloat16


def ring(n):
    return sorted(range(n), key=lambda k: -min(k, n - k))


SNP_OFFSETS = sorted(
    ((a, b) for a in range(Y) for b in range(Z) if (a, b) != (0, 0)),
    key=lambda q: -(min(q[0], Y - q[0]) + min(q[1], Z - q[1])),
)
ALL_OFFSETS = sorted(
    ((a, b, c, d) for a in range(X) for b in range(Y) for c in range(Z) for d in range(2)),
    key=lambda q: -(min(q[0], X - q[0]) + min(q[1], Y - q[1]) + min(q[2], Z - q[2])) - q[3] / 2,
)[:-1]
IND_OFFSETS = [(a, c) for a in ring(X) for c in (1, 0) if (a, c) != (0, 0)]


def split(value):
    high = value.astype(BF16).astype(F32)
    return jnp.concatenate([high, value - high], axis=0).astype(BF16)


def fold(out):
    return out[0:8, 0:BLK] + out[8:16, 0:BLK] + out[0:8, BLK:] + out[8:16, BLK:]


def window(padded, first, width, shift):
    segment = padded[:, first : first + width + BLK]
    return split(pltpu.roll(segment, width + BLK - shift, 1)[:, :width])


def product(b, vec, k0, hilo):
    out = lax.dot_general(
        vec, hilo[b, :, k0 : k0 + vec.shape[1]], NT, preferred_element_type=F32
    )
    return fold(out)


def local_part(value, shifts, hilo, acc):
    empty = jnp.zeros((TR, HALO), F32)
    padded = jnp.concatenate([empty, value, empty], axis=1)
    for b in range(NB):
        k0, k1 = max(0, 384 - BLK * b), min(COLS, 1536 - BLK * b)
        vec = window(padded, BLK * b + k0, k1 - k0, shifts[b])
        acc[:, b * BLK : (b + 1) * BLK] = product(b, vec, k0, hilo)


def halo_part(left, right, shifts, hilo, acc):
    empty = jnp.zeros((TR, BLK), F32)
    left = jnp.concatenate([left, empty], axis=1)
    right = jnp.concatenate([empty, right], axis=1)
    for b in range(NB):
        if b < 4:
            k0 = 0
            vec = window(left, BLK * b, HALO - BLK * b, shifts[b])
        else:
            k0 = 1408 - BLK * b
            vec = window(right, 0, COLS - k0, shifts[b])
        acc[:, b * BLK : (b + 1) * BLK] += product(b, vec, k0, hilo)


def wait_for(ref, sem):
    pltpu.make_async_copy(ref, ref, sem).wait()


def row_sum(value):
    return jnp.sum(value, axis=0, keepdims=True)


def lane_sum(value):
    return jnp.sum(value, axis=1, keepdims=True)


def kernel(
    start_hbm,
    herit_hbm,
    beta_hbm,
    ld_ref,
    geno_ref,
    weights_out,
    scores_out,
    start_ref,
    herit_ref,
    beta_ref,
    ldbuf,
    hilo,
    geno,
    acc,
    ubuf,
    halo,
    basis,
    mom_own,
    mom_in,
    coef_own,
    coef_in,
    part,
    part_in,
    lines_in,
    line_own,
    line_in,
    stat_own,
    stat_in,
    weights_ref,
    scores_ref,
    ld_sem,
    geno_sem,
    small_sem,
    out_sem,
    halo_send,
    halo_recv,
    send_sem,
    recv_sem,
    word,
):
    s, i = lax.axis_index("snp"), lax.axis_index("ind")
    y, z, x, core = s // Z, s % Z, i // 2, i % 2

    def snp_peer(dy, dz):
        return lax.rem(y + dy, Y) * Z + lax.rem(z + dz, Z)

    def ind_peer(dx, dc):
        return lax.rem(x + dx, X) * 2 + lax.rem(core + dc, 2)

    everyone = [
        (snp_peer(dy, dz), ind_peer(dx, dc)) for dx, dy, dz, dc in ALL_OFFSETS
    ]

    def load(b):
        return pltpu.make_async_copy(ld_ref.at[pl.ds(b * BLK, BLK)], ldbuf.at[b], ld_sem.at[b])

    barrier = pltpu.get_barrier_semaphore()
    right, left = lax.rem(s + 1, SNP), lax.rem(s + SNP - 1, SNP)
    around_z = [(snp_peer(0, 1), i), (snp_peer(0, Z - 1), i)]
    around_y = [(snp_peer(dy, 0), i) for dy in range(1, Y)]
    beside = [(s, ind_peer(dx, dc)) for dx, dc in IND_OFFSETS]

    def signal(sem, peer):
        pl.semaphore_signal(sem, inc=1, device_id=peer, device_id_type=MESH)

    for peer in around_z + around_y + beside:
        signal(barrier, peer)

    @pl.when(z == Z - 1)
    def _():
        signal(barrier, (right, i))

    @pl.when(z == 0)
    def _():
        signal(barrier, (left, i))

    small = [
        pltpu.make_async_copy(src, dst, small_sem.at[k])
        for k, (src, dst) in enumerate(
            ((beta_hbm, beta_ref), (start_hbm, start_ref), (herit_hbm, herit_ref))
        )
    ]
    for copy in small:
        copy.start()
    for b in range(NB):
        load(b).start()
    load_geno = pltpu.make_async_copy(geno_ref, geno, geno_sem)
    load_geno.start()

    ends = jnp.where(lax.rem(z + 1, Z) < 2, 1, 0)
    pl.semaphore_wait(barrier, len(around_z + around_y + beside) + ends)

    steps = [
        around_z,
        [(snp_peer(0, 2), i), (snp_peer(0, Z - 2), i)],
        around_y,
    ]

    def tell(step):
        for peer in steps[step]:
            signal(word.at[step], peer)

    def hear(step):
        pl.semaphore_wait(word.at[step], len(steps[step]))

    tell(0)

    for copy in small:
        copy.wait()
    def send_halo(src, turn):
        copies = [
            pltpu.make_async_remote_copy(
                src_ref=src.at[:, COLS - HALO :],
                dst_ref=halo.at[turn, 0],
                send_sem=halo_send.at[turn, 0],
                recv_sem=halo_recv.at[turn, 0],
                device_id=(right, i),
                device_id_type=MESH,
            ),
            pltpu.make_async_remote_copy(
                src_ref=src.at[:, :HALO],
                dst_ref=halo.at[turn, 1],
                send_sem=halo_send.at[turn, 1],
                recv_sem=halo_recv.at[turn, 1],
                device_id=(left, i),
                device_id_type=MESH,
            ),
        ]
        for copy in copies:
            copy.start()
            pending.append(copy.wait_send)
        return copies

    pending = []
    halo0 = send_halo(beta_ref, 0)
    beta = beta_ref[...]

    def gather(turn, parts):
        basis[turn, i] = parts
        for dx, dc in IND_OFFSETS:
            pltpu.make_async_remote_copy(
                src_ref=basis.at[turn, i],
                dst_ref=basis.at[turn, i],
                send_sem=send_sem.at[turn],
                recv_sem=recv_sem.at[turn],
                device_id=(s, ind_peer(dx, dc)),
                device_id_type=MESH,
            ).start()
        pending.append(lambda: wait_for(basis.at[turn, 0 : len(IND_OFFSETS)], send_sem.at[turn]))

    beta_parts = split(beta)
    gather(0, beta_parts)

    shifts = [start_ref[b] - (BLK * (s * NB + b) - HALO) for b in range(NB)]
    for b in range(NB):
        load(b).wait()

        def rows(k, carry, b=b):
            r0 = pl.multiple_of(k * 32, 32)
            value = ldbuf[b, pl.ds(r0, 32), :]
            high = value.astype(BF16)
            hilo[b, pl.ds(r0, 32), :] = high
            hilo[b, pl.ds(BLK + r0, 32), :] = (value - high.astype(F32)).astype(BF16)
            return carry

        lax.fori_loop(0, BLK // 32, rows, 0)

    def off_diagonal(parts, turn, copies):
        for copy in copies:
            copy.wait_recv()
        halo_part(halo[turn, 0], halo[turn, 1], shifts, hilo, acc)
        return acc[...] - (parts[0:8].astype(F32) + parts[8:16].astype(F32))

    local_part(beta, shifts, hilo, acc)
    hear(0)
    tell(1)
    u = off_diagonal(beta_parts, 0, halo0)
    u_parts = split(u)
    gather(1, u_parts)
    ubuf[...] = u
    halo1 = send_halo(ubuf, 1)
    hear(1)
    tell(2)

    slot = {offset: j for j, offset in enumerate(SNP_OFFSETS)}
    lane = lax.broadcasted_iota(jnp.int32, (1, BLK), 1)
    half = lane < 64

    def both(value):
        return value + pltpu.roll(value, 64, value.ndim - 1)

    def partial_scores(turn):
        wait_for(basis.at[turn, 0 : len(IND_OFFSETS)], recv_sem.at[turn])
        every = basis[turn].astype(F32)
        every = jnp.concatenate(
            [every[:, 0:8].reshape(64, COLS), every[:, 8:16].reshape(64, COLS)], axis=0
        ).astype(BF16)
        for dy in ring(Y):
            group = lax.rem(y + dy, Y)
            rows = geno[pl.ds(pl.multiple_of(group * 256, 256), 256), :]
            out = both(lax.dot_general(rows, every, NT, preferred_element_type=F32))
            out = out.reshape(Z, 2, 16, BLK)
            part[turn, pl.ds(group * Z, Z)] = jnp.where(half, out[:, 0], out[:, 1])
            if turn == 0:
                if dy:
                    along_y(dy)
                continue
            for dz in ring(Z):
                if (dy, dz) != (0, 0):
                    peer = group * Z + lax.rem(z + dz, Z)
                    pltpu.make_async_remote_copy(
                        src_ref=part.at[turn, peer],
                        dst_ref=part_in.at[slot[dy, dz]],
                        send_sem=send_sem.at[3],
                        recv_sem=recv_sem.at[3],
                        device_id=(peer, i),
                        device_id_type=MESH,
                    ).start()
        if turn == 1:
            pending.append(lambda: wait_for(part_in, send_sem.at[3]))

    def along_y(dy):
        group = lax.rem(y + dy, Y)
        pltpu.make_async_remote_copy(
            src_ref=part.at[0, pl.ds(group * Z, Z)],
            dst_ref=lines_in.at[dy - 1],
            send_sem=send_sem.at[2],
            recv_sem=recv_sem.at[2],
            device_id=(group * Z + z, i),
            device_id_type=MESH,
        ).start()

    def along_z():
        wait_for(lines_in, recv_sem.at[2])
        line_own[...] = part[0, pl.ds(y * Z, Z)] + jnp.sum(lines_in[...], axis=0)
        for dz in ring(Z)[:-1]:
            peer = lax.rem(z + dz, Z)
            pltpu.make_async_remote_copy(
                src_ref=line_own.at[peer],
                dst_ref=line_in.at[dz - 1],
                send_sem=send_sem.at[8],
                recv_sem=recv_sem.at[8],
                device_id=(y * Z + peer, i),
                device_id_type=MESH,
            ).start()
        pending.append(lambda: wait_for(lines_in, send_sem.at[2]))
        pending.append(lambda: wait_for(line_in, send_sem.at[8]))

    def total_scores(turn):
        if turn == 0:
            wait_for(line_in, recv_sem.at[8])
            return line_own[z] + jnp.sum(line_in[...], axis=0)
        wait_for(part_in, recv_sem.at[3])
        return part[1, s] + jnp.sum(part_in[...], axis=0)

    load_geno.wait()
    partial_scores(0)

    local_part(u, shifts, hilo, acc)
    p0 = lane_sum(beta * beta)
    p1 = lane_sum(beta * u)
    theta = jnp.where(p0 > 0, p1 / p0, 0.0)
    e = u - theta * beta
    q = lane_sum(e * e)
    t = lane_sum(e * beta)

    g = off_diagonal(u_parts, 1, halo1) - theta * u
    f = lane_sum(e * g)
    h = lane_sum(beta * g)
    tile_lane = lax.broadcasted_iota(jnp.int32, (TR, BLK), 1)
    tile_row = lax.broadcasted_iota(jnp.int32, (TR, BLK), 0)
    tile = jnp.broadcast_to(p0, (TR, BLK))
    for k, value in enumerate((theta, q, t, f, h)):
        tile = jnp.where(tile_lane >= 16 * (k + 1), value, tile)
    tile = jnp.where(tile_lane % 16 == tile_row, tile, 0.0)
    sums = jnp.sum(tile, axis=0, keepdims=True)
    hear(2)
    mom_own[...] = sums
    mom_in[SNP - 1 :] = sums
    for j, (dy, dz) in enumerate(SNP_OFFSETS):
        pltpu.make_async_remote_copy(
            src_ref=mom_own,
            dst_ref=mom_in.at[pl.ds(j, 1)],
            send_sem=send_sem.at[4],
            recv_sem=recv_sem.at[4],
            device_id=(snp_peer(dy, dz), i),
            device_id_type=MESH,
        ).start()

    pending.append(lambda: wait_for(mom_in.at[0 : len(SNP_OFFSETS)], send_sem.at[4]))

    partial_scores(1)
    along_z()

    herit = jnp.ones((1, BLK), F32)
    for k in range(TR):
        herit = jnp.where(lane == k, herit_ref[k], herit)
    kappa = 1.0 + (M_GENOME / N_GWAS) / herit

    wait_for(mom_in.at[0 : len(SNP_OFFSETS)], recv_sem.at[4])
    moments = mom_in[...]
    p0_d, th_d, q_d, t_d, f_d, h_d = [
        moments if k == 0 else pltpu.roll(moments, BLK - 16 * k, 1) for k in range(6)
    ]
    p0 = row_sum(p0_d)
    theta = row_sum(p0_d * th_d + t_d) / p0
    delta = th_d - theta
    q = row_sum(q_d + delta * (2.0 * t_d + delta * p0_d))
    t = row_sum(t_d + delta * p0_d)
    f = row_sum(f_d + delta * (q_d + th_d * t_d + h_d + delta * (t_d + th_d * p0_d)))
    a11 = p0 * (theta + kappa)
    a12 = q + (theta + kappa) * t
    a22 = f + kappa * q
    ratio = a12 / a11
    rest = a22 - a12 * ratio
    c1 = jnp.where(rest > 0, (t - p0 * ratio) / rest, 0.0)
    c0 = p0 / a11 - c1 * (ratio + theta)

    own_lanes = lane < TR
    coef = jnp.where(own_lanes, c0, 0.0) + pltpu.roll(jnp.where(own_lanes, c1, 0.0), 64, 1)
    coef = pltpu.roll(coef, i * TR, 1)
    coef_own[...] = coef
    coef_in[IND - 1 :] = coef
    for j, (dx, dc) in enumerate(IND_OFFSETS):
        pltpu.make_async_remote_copy(
            src_ref=coef_own,
            dst_ref=coef_in.at[pl.ds(j, 1)],
            send_sem=send_sem.at[5],
            recv_sem=recv_sem.at[5],
            device_id=(s, ind_peer(dx, dc)),
            device_id_type=MESH,
        ).start()

    pending.append(lambda: wait_for(coef_in.at[0 : len(IND_OFFSETS)], send_sem.at[5]))

    diagonal = tile_lane == tile_row
    c0 = lane_sum(jnp.where(diagonal, c0, 0.0))
    c1 = lane_sum(jnp.where(diagonal, c1, 0.0))
    weights_ref[...] = c0 * beta + c1 * u
    store_weights = pltpu.make_async_copy(weights_ref, weights_out, out_sem.at[0])
    store_weights.start()

    beta_scores = total_scores(0)
    wait_for(coef_in.at[0 : len(IND_OFFSETS)], recv_sem.at[5])
    coef = row_sum(coef_in[...])
    swapped = pltpu.roll(coef, 64, 1)
    beta_scores = beta_scores * jnp.where(half, coef, swapped)
    raw = beta_scores + total_scores(1) * jnp.where(half, swapped, coef)

    mean = both(jnp.sum(raw, axis=0, keepdims=True)) * (1.0 / SHARE)
    spread = both(jnp.sum((raw - mean) * (raw - mean), axis=0, keepdims=True))
    stat = jnp.where(half, mean, spread)
    count = len(everyone) + 1
    stat_own[...] = stat
    stat_in[len(everyone) :] = stat
    for j, peer in enumerate(everyone):
        pltpu.make_async_remote_copy(
            src_ref=stat_own,
            dst_ref=stat_in.at[pl.ds(j, 1)],
            send_sem=send_sem.at[6],
            recv_sem=recv_sem.at[6],
            device_id=peer,
            device_id_type=MESH,
        ).start()
    arrived = stat_in.at[0 : len(everyone)]
    pending.append(lambda: wait_for(arrived, send_sem.at[6]))
    wait_for(arrived, recv_sem.at[6])
    values = stat_in[...]
    total = row_sum(values)
    mean = total * (1.0 / count)
    apart = jnp.where(half, values - mean, 0.0)
    squares = row_sum(apart * apart) * float(SHARE)
    stat = jnp.where(half, mean, total + pltpu.roll(squares, 64, 1))
    size = SHARE * count
    swapped = pltpu.roll(stat, 64, 1)
    mean = jnp.where(half, stat, swapped)
    variance = jnp.where(half, swapped, stat) * (1.0 / size)
    scores = (raw - mean) * lax.rsqrt(variance + 1e-05)
    scores_ref[0:16, :] = scores[:, 0:64]
    scores_ref[16:32, :] = scores[:, 64:128]
    store_scores = pltpu.make_async_copy(scores_ref, scores_out, out_sem.at[1])
    store_scores.start()

    for drain in pending:
        drain()
    store_weights.wait()
    store_scores.wait()


def hand_over(weights_ref, scores_ref, weights_out, scores_out):
    weights_out[...] = weights_ref[...]
    scores_out[...] = scores_ref[...]


def local(beta_hat, ld_band, band_start, heritability, genotypes):
    vmem, anywhere = pl.BlockSpec(memory_space=pltpu.VMEM), pl.BlockSpec(memory_space=pl.ANY)
    dma = pltpu.SemaphoreType.DMA
    weights, scores = pl.pallas_call(
        kernel,
        out_shape=(
            jax.ShapeDtypeStruct((TR, COLS), F32),
            jax.ShapeDtypeStruct((SHARE, 64), F32),
        ),
        in_specs=[anywhere] * 5,
        out_specs=(anywhere, anywhere),
        scratch_shapes=[
            pltpu.SMEM((NB,), jnp.int32),
            pltpu.SMEM((TR,), F32),
            pltpu.VMEM((TR, COLS), F32),
            pltpu.VMEM((NB, BLK, COLS), F32),
            pltpu.VMEM((NB, 2 * BLK, COLS), BF16),
            pltpu.VMEM((1024, COLS), BF16),
            pltpu.VMEM((TR, COLS), F32),
            pltpu.VMEM((TR, COLS), F32),
            pltpu.VMEM((2, 2, TR, HALO), F32),
            pltpu.VMEM((2, IND, 16, COLS), BF16),
            pltpu.VMEM((1, BLK), F32),
            pltpu.VMEM((SNP, BLK), F32),
            pltpu.VMEM((1, BLK), F32),
            pltpu.VMEM((IND, BLK), F32),
            pltpu.VMEM((2, SNP, 16, BLK), F32),
            pltpu.VMEM((SNP - 1, 16, BLK), F32),
            pltpu.VMEM((Y - 1, Z, 16, BLK), F32),
            pltpu.VMEM((Z, 16, BLK), F32),
            pltpu.VMEM((Z - 1, 16, BLK), F32),
            pltpu.VMEM((1, BLK), F32),
            pltpu.VMEM((SNP * IND, BLK), F32),
            pltpu.VMEM((TR, COLS), F32),
            pltpu.VMEM((SHARE, 64), F32),
            dma((NB,)),
            dma,
            dma((3,)),
            dma((2,)),
            dma((2, 2)),
            dma((2, 2)),
            dma((9,)),
            dma((9,)),
            pltpu.SemaphoreType.REGULAR((3,)),
        ],
        name="ldpred_scores",
        compiler_params=pltpu.CompilerParams(
            collective_id=0, has_side_effects=True, vmem_limit_bytes=60 << 20
        ),
    )(band_start, heritability, beta_hat, ld_band, genotypes)
    weights, scores = pl.pallas_call(
        hand_over,
        out_shape=(
            jax.ShapeDtypeStruct((TR, COLS), F32),
            jax.ShapeDtypeStruct((SHARE, 64), F32),
        ),
        in_specs=[vmem] * 2,
        out_specs=(vmem, vmem),
        name="hand_over",
        compiler_params=pltpu.CompilerParams(vmem_limit_bytes=60 << 20),
    )(weights, scores)
    return weights, scores.T


def solution(mesh):
    placed = (P("ind", "snp"), P("snp", None), P("snp"), P("ind"), P("ind", "snp"))
    return jax.shard_map(
        local,
        mesh=mesh,
        in_specs=placed,
        out_specs=(P("ind", "snp"), P(None, ("ind", "snp"))),
        check_vma=False,
    )
```

```python
import functools

import jax
import jax.numpy as jnp
from jax import lax
from jax.experimental import pallas as pl
from jax.experimental.pallas import tpu as pltpu
from jax.sharding import PartitionSpec as P

BLK = 128
M_GENOME = 1100000
N_GWAS = 1000000
SNP, IND = 32, 8
Y, Z, X = 4, 8, 4
NB = 8
TR = 8
COLS = NB * BLK
HALO = 512
SHARE = 32
MESH = pl.DeviceIdType.MESH
NT = (((1,), (1,)), ((), ()))
F32, BF16 = jnp.float32, jnp.bfloat16


def ring(n):
    return sorted(range(n), key=lambda k: -min(k, n - k))


SNP_OFFSETS = sorted(
    ((a, b) for a in range(Y) for b in range(Z) if (a, b) != (0, 0)),
    key=lambda q: -(min(q[0], Y - q[0]) + min(q[1], Z - q[1])),
)
ALL_OFFSETS = sorted(
    ((a, b, c, d) for a in range(X) for b in range(Y) for c in range(Z) for d in range(2)),
    key=lambda q: -(min(q[0], X - q[0]) + min(q[1], Y - q[1]) + min(q[2], Z - q[2])) - q[3] / 2,
)[:-1]
IND_OFFSETS = [(a, c) for a in ring(X) for c in (1, 0) if (a, c) != (0, 0)]


def split(value):
    high = value.astype(BF16).astype(F32)
    return jnp.concatenate([high, value - high], axis=0).astype(BF16)


def fold(out):
    return out[0:8, 0:BLK] + out[8:16, 0:BLK] + out[0:8, BLK:] + out[8:16, BLK:]


def window(padded, first, width, shift):
    segment = padded[:, first : first + width + BLK]
    return split(pltpu.roll(segment, width + BLK - shift, 1)[:, :width])


def product(b, vec, k0, hilo):
    out = lax.dot_general(
        vec, hilo[b, :, k0 : k0 + vec.shape[1]], NT, preferred_element_type=F32
    )
    return fold(out)


def local_part(value, shifts, hilo, acc):
    empty = jnp.zeros((TR, HALO), F32)
    padded = jnp.concatenate([empty, value, empty], axis=1)
    for b in range(NB):
        k0, k1 = max(0, 384 - BLK * b), min(COLS, 1536 - BLK * b)
        vec = window(padded, BLK * b + k0, k1 - k0, shifts[b])
        acc[:, b * BLK : (b + 1) * BLK] = product(b, vec, k0, hilo)


def halo_part(left, right, shifts, hilo, acc):
    empty = jnp.zeros((TR, BLK), F32)
    left = jnp.concatenate([left, empty], axis=1)
    right = jnp.concatenate([empty, right], axis=1)
    for b in range(NB):
        if b < 4:
            k0 = 0
            vec = window(left, BLK * b, HALO - BLK * b, shifts[b])
        else:
            k0 = 1408 - BLK * b
            vec = window(right, 0, COLS - k0, shifts[b])
        acc[:, b * BLK : (b + 1) * BLK] += product(b, vec, k0, hilo)


def wait_for(ref, sem):
    pltpu.make_async_copy(ref, ref, sem).wait()


def row_sum(value):
    return jnp.sum(value, axis=0, keepdims=True)


def lane_sum(value):
    return jnp.sum(value, axis=1, keepdims=True)


def kernel(
    start_hbm,
    herit_hbm,
    beta_hbm,
    ld_ref,
    geno_ref,
    weights_out,
    scores_out,
    start_ref,
    herit_ref,
    beta_ref,
    ldbuf,
    hilo,
    geno,
    acc,
    ubuf,
    halo,
    basis,
    mom_own,
    mom_in,
    coef_own,
    coef_in,
    part,
    part_in,
    lines_in,
    line_own,
    line_in,
    stat_own,
    stat_in,
    weights_ref,
    scores_ref,
    ld_sem,
    geno_sem,
    small_sem,
    out_sem,
    halo_send,
    halo_recv,
    send_sem,
    recv_sem,
    word,
):
    s, i = lax.axis_index("snp"), lax.axis_index("ind")
    y, z, x, core = s // Z, s % Z, i // 2, i % 2

    def snp_peer(dy, dz):
        return lax.rem(y + dy, Y) * Z + lax.rem(z + dz, Z)

    def ind_peer(dx, dc):
        return lax.rem(x + dx, X) * 2 + lax.rem(core + dc, 2)

    everyone = [
        (snp_peer(dy, dz), ind_peer(dx, dc)) for dx, dy, dz, dc in ALL_OFFSETS
    ]

    def load(b):
        return pltpu.make_async_copy(ld_ref.at[pl.ds(b * BLK, BLK)], ldbuf.at[b], ld_sem.at[b])

    barrier = pltpu.get_barrier_semaphore()
    right, left = lax.rem(s + 1, SNP), lax.rem(s + SNP - 1, SNP)
    around_z = [(snp_peer(0, 1), i), (snp_peer(0, Z - 1), i)]
    around_y = [(snp_peer(dy, 0), i) for dy in range(1, Y)]
    beside = [(s, ind_peer(dx, dc)) for dx, dc in IND_OFFSETS]

    def signal(sem, peer):
        pl.semaphore_signal(sem, inc=1, device_id=peer, device_id_type=MESH)

    for peer in around_z + around_y + beside:
        signal(barrier, peer)

    @pl.when(z == Z - 1)
    def _():
        signal(barrier, (right, i))

    @pl.when(z == 0)
    def _():
        signal(barrier, (left, i))

    small = [
        pltpu.make_async_copy(src, dst, small_sem.at[k])
        for k, (src, dst) in enumerate(
            ((beta_hbm, beta_ref), (start_hbm, start_ref), (herit_hbm, herit_ref))
        )
    ]
    for copy in small:
        copy.start()
    for b in range(NB):
        load(b).start()
    load_geno = pltpu.make_async_copy(geno_ref, geno, geno_sem)
    load_geno.start()

    ends = jnp.where(lax.rem(z + 1, Z) < 2, 1, 0)
    pl.semaphore_wait(barrier, len(around_z + around_y + beside) + ends)

    steps = [
        around_z,
        [(snp_peer(0, 2), i), (snp_peer(0, Z - 2), i)],
        around_y,
    ]

    def tell(step):
        for peer in steps[step]:
            signal(word.at[step], peer)

    def hear(step):
        pl.semaphore_wait(word.at[step], len(steps[step]))

    tell(0)

    for copy in small:
        copy.wait()
    def send_halo(src, turn):
        copies = [
            pltpu.make_async_remote_copy(
                src_ref=src.at[:, COLS - HALO :],
                dst_ref=halo.at[turn, 0],
                send_sem=halo_send.at[turn, 0],
                recv_sem=halo_recv.at[turn, 0],
                device_id=(right, i),
                device_id_type=MESH,
            ),
            pltpu.make_async_remote_copy(
                src_ref=src.at[:, :HALO],
                dst_ref=halo.at[turn, 1],
                send_sem=halo_send.at[turn, 1],
                recv_sem=halo_recv.at[turn, 1],
                device_id=(left, i),
                device_id_type=MESH,
            ),
        ]
        for copy in copies:
            copy.start()
            pending.append(copy.wait_send)
        return copies

    pending = []
    halo0 = send_halo(beta_ref, 0)
    beta = beta_ref[...]

    def gather(turn, parts):
        basis[turn, i] = parts
        for dx, dc in IND_OFFSETS:
            pltpu.make_async_remote_copy(
                src_ref=basis.at[turn, i],
                dst_ref=basis.at[turn, i],
                send_sem=send_sem.at[turn],
                recv_sem=recv_sem.at[turn],
                device_id=(s, ind_peer(dx, dc)),
                device_id_type=MESH,
            ).start()
        pending.append(lambda: wait_for(basis.at[turn, 0 : len(IND_OFFSETS)], send_sem.at[turn]))

    beta_parts = split(beta)
    gather(0, beta_parts)

    shifts = [start_ref[b] - (BLK * (s * NB + b) - HALO) for b in range(NB)]
    for b in range(NB):
        load(b).wait()

        def rows(k, carry, b=b):
            r0 = pl.multiple_of(k * 32, 32)
            value = ldbuf[b, pl.ds(r0, 32), :]
            high = value.astype(BF16)
            hilo[b, pl.ds(r0, 32), :] = high
            hilo[b, pl.ds(BLK + r0, 32), :] = (value - high.astype(F32)).astype(BF16)
            return carry

        lax.fori_loop(0, BLK // 32, rows, 0)

    def off_diagonal(parts, turn, copies):
        for copy in copies:
            copy.wait_recv()
        halo_part(halo[turn, 0], halo[turn, 1], shifts, hilo, acc)
        return acc[...] - (parts[0:8].astype(F32) + parts[8:16].astype(F32))

    local_part(beta, shifts, hilo, acc)
    hear(0)
    tell(1)
    u = off_diagonal(beta_parts, 0, halo0)
    u_parts = split(u)
    gather(1, u_parts)
    ubuf[...] = u
    halo1 = send_halo(ubuf, 1)
    hear(1)
    tell(2)

    slot = {offset: j for j, offset in enumerate(SNP_OFFSETS)}
    lane = lax.broadcasted_iota(jnp.int32, (1, BLK), 1)
    half = lane < 64

    def both(value):
        return value + pltpu.roll(value, 64, value.ndim - 1)

    def partial_scores(turn):
        wait_for(basis.at[turn, 0 : len(IND_OFFSETS)], recv_sem.at[turn])
        every = basis[turn].astype(F32)
        every = jnp.concatenate(
            [every[:, 0:8].reshape(64, COLS), every[:, 8:16].reshape(64, COLS)], axis=0
        ).astype(BF16)
        for dy in ring(Y):
            group = lax.rem(y + dy, Y)
            rows = geno[pl.ds(pl.multiple_of(group * 256, 256), 256), :]
            out = both(lax.dot_general(rows, every, NT, preferred_element_type=F32))
            out = out.reshape(Z, 2, 16, BLK)
            part[turn, pl.ds(group * Z, Z)] = jnp.where(half, out[:, 0], out[:, 1])
            if turn == 0:
                if dy:
                    along_y(dy)
                continue
            for dz in ring(Z):
                if (dy, dz) != (0, 0):
                    peer = group * Z + lax.rem(z + dz, Z)
                    pltpu.make_async_remote_copy(
                        src_ref=part.at[turn, peer],
                        dst_ref=part_in.at[slot[dy, dz]],
                        send_sem=send_sem.at[3],
                        recv_sem=recv_sem.at[3],
                        device_id=(peer, i),
                        device_id_type=MESH,
                    ).start()
        if turn == 1:
            pending.append(lambda: wait_for(part_in, send_sem.at[3]))

    def along_y(dy):
        group = lax.rem(y + dy, Y)
        pltpu.make_async_remote_copy(
            src_ref=part.at[0, pl.ds(group * Z, Z)],
            dst_ref=lines_in.at[dy - 1],
            send_sem=send_sem.at[2],
            recv_sem=recv_sem.at[2],
            device_id=(group * Z + z, i),
            device_id_type=MESH,
        ).start()

    def along_z():
        wait_for(lines_in, recv_sem.at[2])
        line_own[...] = part[0, pl.ds(y * Z, Z)] + jnp.sum(lines_in[...], axis=0)
        for dz in ring(Z)[:-1]:
            peer = lax.rem(z + dz, Z)
            pltpu.make_async_remote_copy(
                src_ref=line_own.at[peer],
                dst_ref=line_in.at[dz - 1],
                send_sem=send_sem.at[8],
                recv_sem=recv_sem.at[8],
                device_id=(y * Z + peer, i),
                device_id_type=MESH,
            ).start()
        pending.append(lambda: wait_for(lines_in, send_sem.at[2]))
        pending.append(lambda: wait_for(line_in, send_sem.at[8]))

    def total_scores(turn):
        if turn == 0:
            wait_for(line_in, recv_sem.at[8])
            return line_own[z] + jnp.sum(line_in[...], axis=0)
        wait_for(part_in, recv_sem.at[3])
        return part[1, s] + jnp.sum(part_in[...], axis=0)

    load_geno.wait()
    partial_scores(0)

    local_part(u, shifts, hilo, acc)
    p0 = lane_sum(beta * beta)
    p1 = lane_sum(beta * u)
    theta = jnp.where(p0 > 0, p1 / p0, 0.0)
    e = u - theta * beta
    q = lane_sum(e * e)
    t = lane_sum(e * beta)

    g = off_diagonal(u_parts, 1, halo1) - theta * u
    f = lane_sum(e * g)
    h = lane_sum(beta * g)
    tile_lane = lax.broadcasted_iota(jnp.int32, (TR, BLK), 1)
    tile_row = lax.broadcasted_iota(jnp.int32, (TR, BLK), 0)
    tile = jnp.broadcast_to(p0, (TR, BLK))
    for k, value in enumerate((theta, q, t, f, h)):
        tile = jnp.where(tile_lane >= 16 * (k + 1), value, tile)
    tile = jnp.where(tile_lane % 16 == tile_row, tile, 0.0)
    sums = jnp.sum(tile, axis=0, keepdims=True)
    hear(2)
    mom_own[...] = sums
    mom_in[SNP - 1 :] = sums
    for j, (dy, dz) in enumerate(SNP_OFFSETS):
        pltpu.make_async_remote_copy(
            src_ref=mom_own,
            dst_ref=mom_in.at[pl.ds(j, 1)],
            send_sem=send_sem.at[4],
            recv_sem=recv_sem.at[4],
            device_id=(snp_peer(dy, dz), i),
            device_id_type=MESH,
        ).start()

    pending.append(lambda: wait_for(mom_in.at[0 : len(SNP_OFFSETS)], send_sem.at[4]))

    partial_scores(1)
    along_z()

    herit = jnp.ones((1, BLK), F32)
    for k in range(TR):
        herit = jnp.where(lane == k, herit_ref[k], herit)
    kappa = 1.0 + (M_GENOME / N_GWAS) / herit

    wait_for(mom_in.at[0 : len(SNP_OFFSETS)], recv_sem.at[4])
    moments = mom_in[...]
    p0_d, th_d, q_d, t_d, f_d, h_d = [
        moments if k == 0 else pltpu.roll(moments, BLK - 16 * k, 1) for k in range(6)
    ]
    p0 = row_sum(p0_d)
    theta = row_sum(p0_d * th_d + t_d) / p0
    delta = th_d - theta
    q = row_sum(q_d + delta * (2.0 * t_d + delta * p0_d))
    t = row_sum(t_d + delta * p0_d)
    f = row_sum(f_d + delta * (q_d + th_d * t_d + h_d + delta * (t_d + th_d * p0_d)))
    a11 = p0 * (theta + kappa)
    a12 = q + (theta + kappa) * t
    a22 = f + kappa * q
    ratio = a12 / a11
    rest = a22 - a12 * ratio
    c1 = jnp.where(rest > 0, (t - p0 * ratio) / rest, 0.0)
    c0 = p0 / a11 - c1 * (ratio + theta)

    own_lanes = lane < TR
    coef = jnp.where(own_lanes, c0, 0.0) + pltpu.roll(jnp.where(own_lanes, c1, 0.0), 64, 1)
    coef = pltpu.roll(coef, i * TR, 1)
    coef_own[...] = coef
    coef_in[IND - 1 :] = coef
    for j, (dx, dc) in enumerate(IND_OFFSETS):
        pltpu.make_async_remote_copy(
            src_ref=coef_own,
            dst_ref=coef_in.at[pl.ds(j, 1)],
            send_sem=send_sem.at[5],
            recv_sem=recv_sem.at[5],
            device_id=(s, ind_peer(dx, dc)),
            device_id_type=MESH,
        ).start()

    pending.append(lambda: wait_for(coef_in.at[0 : len(IND_OFFSETS)], send_sem.at[5]))

    diagonal = tile_lane == tile_row
    c0 = lane_sum(jnp.where(diagonal, c0, 0.0))
    c1 = lane_sum(jnp.where(diagonal, c1, 0.0))
    weights_ref[...] = c0 * beta + c1 * u
    store_weights = pltpu.make_async_copy(weights_ref, weights_out, out_sem.at[0])
    store_weights.start()

    beta_scores = total_scores(0)
    wait_for(coef_in.at[0 : len(IND_OFFSETS)], recv_sem.at[5])
    coef = row_sum(coef_in[...])
    swapped = pltpu.roll(coef, 64, 1)
    beta_scores = beta_scores * jnp.where(half, coef, swapped)
    raw = beta_scores + total_scores(1) * jnp.where(half, swapped, coef)

    mean = both(jnp.sum(raw, axis=0, keepdims=True)) * (1.0 / SHARE)
    spread = both(jnp.sum((raw - mean) * (raw - mean), axis=0, keepdims=True))
    stat = jnp.where(half, mean, spread)
    count = len(everyone) + 1
    stat_own[...] = stat
    stat_in[len(everyone) :] = stat
    for j, peer in enumerate(everyone):
        pltpu.make_async_remote_copy(
            src_ref=stat_own,
            dst_ref=stat_in.at[pl.ds(j, 1)],
            send_sem=send_sem.at[6],
            recv_sem=recv_sem.at[6],
            device_id=peer,
            device_id_type=MESH,
        ).start()
    arrived = stat_in.at[0 : len(everyone)]
    pending.append(lambda: wait_for(arrived, send_sem.at[6]))
    for drain in pending:
        drain()
    store_weights.wait()
    wait_for(arrived, recv_sem.at[6])
    values = stat_in[...]
    total = row_sum(values)
    mean = total * (1.0 / count)
    apart = jnp.where(half, values - mean, 0.0)
    squares = row_sum(apart * apart) * float(SHARE)
    stat = jnp.where(half, mean, total + pltpu.roll(squares, 64, 1))
    size = SHARE * count
    swapped = pltpu.roll(stat, 64, 1)
    mean = jnp.where(half, stat, swapped)
    variance = jnp.where(half, swapped, stat) * (1.0 / size)
    scores = (raw - mean) * lax.rsqrt(variance + 1e-05)
    scores_ref[0:16, :] = scores[:, 0:64]
    scores_ref[16:32, :] = scores[:, 64:128]
    store_scores = pltpu.make_async_copy(scores_ref, scores_out, out_sem.at[1])
    store_scores.start()
    store_scores.wait()


def hand_over(weights_ref, scores_ref, weights_out, scores_out):
    weights_out[...] = weights_ref[...]
    scores_out[...] = scores_ref[...]


def local(beta_hat, ld_band, band_start, heritability, genotypes):
    vmem, anywhere = pl.BlockSpec(memory_space=pltpu.VMEM), pl.BlockSpec(memory_space=pl.ANY)
    dma = pltpu.SemaphoreType.DMA
    weights, scores = pl.pallas_call(
        kernel,
        out_shape=(
            jax.ShapeDtypeStruct((TR, COLS), F32),
            jax.ShapeDtypeStruct((SHARE, 64), F32),
        ),
        in_specs=[anywhere] * 5,
        out_specs=(anywhere, anywhere),
        scratch_shapes=[
            pltpu.SMEM((NB,), jnp.int32),
            pltpu.SMEM((TR,), F32),
            pltpu.VMEM((TR, COLS), F32),
            pltpu.VMEM((NB, BLK, COLS), F32),
            pltpu.VMEM((NB, 2 * BLK, COLS), BF16),
            pltpu.VMEM((1024, COLS), BF16),
            pltpu.VMEM((TR, COLS), F32),
            pltpu.VMEM((TR, COLS), F32),
            pltpu.VMEM((2, 2, TR, HALO), F32),
            pltpu.VMEM((2, IND, 16, COLS), BF16),
            pltpu.VMEM((1, BLK), F32),
            pltpu.VMEM((SNP, BLK), F32),
            pltpu.VMEM((1, BLK), F32),
            pltpu.VMEM((IND, BLK), F32),
            pltpu.VMEM((2, SNP, 16, BLK), F32),
            pltpu.VMEM((SNP - 1, 16, BLK), F32),
            pltpu.VMEM((Y - 1, Z, 16, BLK), F32),
            pltpu.VMEM((Z, 16, BLK), F32),
            pltpu.VMEM((Z - 1, 16, BLK), F32),
            pltpu.VMEM((1, BLK), F32),
            pltpu.VMEM((SNP * IND, BLK), F32),
            pltpu.VMEM((TR, COLS), F32),
            pltpu.VMEM((SHARE, 64), F32),
            dma((NB,)),
            dma,
            dma((3,)),
            dma((2,)),
            dma((2, 2)),
            dma((2, 2)),
            dma((9,)),
            dma((9,)),
            pltpu.SemaphoreType.REGULAR((3,)),
        ],
        name="ldpred_scores",
        compiler_params=pltpu.CompilerParams(
            collective_id=0, has_side_effects=True, vmem_limit_bytes=60 << 20
        ),
    )(band_start, heritability, beta_hat, ld_band, genotypes)
    weights, scores = pl.pallas_call(
        hand_over,
        out_shape=(
            jax.ShapeDtypeStruct((TR, COLS), F32),
            jax.ShapeDtypeStruct((SHARE, 64), F32),
        ),
        in_specs=[vmem] * 2,
        out_specs=(vmem, vmem),
        name="hand_over",
        compiler_params=pltpu.CompilerParams(vmem_limit_bytes=60 << 20),
    )(weights, scores)
    return weights, scores.T


def solution(mesh):
    placed = (P("ind", "snp"), P("snp", None), P("snp"), P("ind"), P("ind", "snp"))
    return jax.shard_map(
        local,
        mesh=mesh,
        in_specs=placed,
        out_specs=(P("ind", "snp"), P(None, ("ind", "snp"))),
        check_vma=False,
    )
```
